256 devices in a mesh: row: 8 (over z_lo, x), col: 32 (over z_hi, y, core).
Axes of the slice: x: 4, y: 4, z: 8 (z_hi: 4, z_lo: 2; z = z_hi * 2 + z_lo), core: 2. Of those that a mesh axis runs over, the one named last changes fastest.
Arguments:
- pair: bfloat16 [1024, 1024, 128], P('row', 'col'), may hold values from -6 to 6
- in_gain: float32 [2, 128], replicated, may hold values from 0.1 to 1.9
- w_in: bfloat16 [2, 128, 512], replicated, may hold values from -0.5 to 0.5
- out_gain: float32 [2, 128], replicated, may hold values from 0.1 to 1.9
- out_bias: float32 [2, 128], replicated, may hold values from -3 to 3
- w_out: bfloat16 [2, 128, 128], replicated, may hold values from -0.5 to 0.5
- w_gate_out: bfloat16 [2, 128, 128], replicated, may hold values from -0.5 to 0.5
Outputs:
- updated: bfloat16 [1024, 1024, 128], P('row', 'col')
The draws below stay inside these ranges and needn't reach their ends.
All inputs are finite; a program needn't handle non-finite values.
Results may differ from the reference program's by a relative error of at most 0.015.
Values may be sent and summed in bfloat16 or wider, within the bound.
A program may use at most 64 MiB of HBM per device.

```python
import jax
import jax.numpy as jnp
from jax import lax

C = 128
CH = 128
N = 1024


def shard_levels(stream_key, extent, shards, least, top_value):
    factor_of = 1.0
    for axis_at, parts in shards:
        steps = jax.random.uniform(jax.random.fold_in(jax.random.fold_in(stream_key, 6), axis_at), (parts,), jnp.float32, least / len(shards), top_value / len(shards))
        factor_of = factor_of * jnp.repeat(jnp.exp(steps), extent[axis_at] // parts).reshape((-1,) + (1,) * (len(extent) - 1 - axis_at))
    return factor_of


def scatter_about(key, shape, deviation, most, pieces=(), held_as=jnp.bfloat16):
    loudness = shard_levels(key, shape, pieces, -0.22, 0.18) if pieces else 1.0
    entries = jax.random.normal(key, shape, jnp.float32) * deviation * loudness
    return jnp.minimum(jnp.maximum(entries, -most), most).astype(held_as)


def setup_inputs(seed: int = 0) -> dict:
    splits = jax.random.split(jax.random.key(seed), 8)
    return {
        "pair": scatter_about(splits[0], (N, N, C), 1.0, 6.0, ((0, 8), (1, 32))),
        "in_gain": jnp.clip(1.0 + 0.18 * jax.random.normal(splits[1], (2, C), jnp.float32), 0.1, 1.9),
        "w_in": scatter_about(splits[2], (2, C, 4 * CH), C ** -0.5, 0.5),
        "out_gain": jnp.clip(1.0 + 0.18 * jax.random.normal(splits[3], (2, CH), jnp.float32), 0.1, 1.9),
        "out_bias": scatter_about(splits[4], (2, CH), 0.5, 3.0, (), jnp.float32),
        "w_out": scatter_about(splits[5], (2, CH, C), CH ** -0.5, 0.5),
        "w_gate_out": scatter_about(splits[6], (2, C, C), C ** -0.5, 0.5),
    }


EPS = 1e-05

def layer_norm(values, gain, bias, axis):
    mean = lax.optimization_barrier(jnp.mean(values, axis=axis, keepdims=True))
    var = lax.optimization_barrier(jnp.mean(jnp.square(values - mean), axis=axis, keepdims=True))
    return (values - mean) * lax.rsqrt(var + EPS) * gain + bias

def triangle(pair, index, in_gain, w_in, out_gain, out_bias, w_out, w_gate_out):
    width = pair.shape[0]
    x = layer_norm(pair.astype(jnp.float32), in_gain[index], 0.0, -1).astype(jnp.bfloat16)
    flat = x.reshape(width * width, C)
    weights = w_in[index]
    pa = jnp.dot(flat, weights[:, 0:CH], preferred_element_type=jnp.float32)
    ga = jnp.dot(flat, weights[:, 2 * CH:3 * CH], preferred_element_type=jnp.float32)
    left = (pa * jax.nn.sigmoid(ga)).astype(jnp.bfloat16).reshape(width, width, CH)
    pb = jnp.dot(flat, weights[:, CH:2 * CH], preferred_element_type=jnp.float32)
    gb = jnp.dot(flat, weights[:, 3 * CH:4 * CH], preferred_element_type=jnp.float32)
    right = (pb * jax.nn.sigmoid(gb)).astype(jnp.bfloat16).reshape(width, width, CH)
    if index == 0:
        prod = jnp.einsum('ikc,jkc->cij', left.astype(jnp.float32), right.astype(jnp.float32))
    else:
        prod = jnp.einsum('kic,kjc->cij', left.astype(jnp.float32), right.astype(jnp.float32))
    normed = layer_norm(prod, out_gain[index][:, None, None], out_bias[index][:, None, None], 0).astype(jnp.bfloat16)
    projected = jnp.einsum('cij,cd->ijd', normed.astype(jnp.float32), w_out[index].astype(jnp.float32))
    gate = jnp.dot(flat, w_gate_out[index], preferred_element_type=jnp.float32).reshape(width, width, C)
    return (pair.astype(jnp.float32) + projected * jax.nn.sigmoid(gate)).astype(jnp.bfloat16)

def reference(pair, in_gain, w_in, out_gain, out_bias, w_out, w_gate_out):
    first = triangle(pair, 0, in_gain, w_in, out_gain, out_bias, w_out, w_gate_out)
    return triangle(first, 1, in_gain, w_in, out_gain, out_bias, w_out, w_gate_out)
```

```python
import functools

import jax
import jax.numpy as jnp
from jax import lax
from jax.experimental import pallas as pl
from jax.experimental.pallas import tpu as pltpu
from jax.sharding import PartitionSpec as P

EPS = 1e-05
MESH = pl.DeviceIdType.MESH
CHIPS = 128


def chip_of(x, y, z):
    return x * 32 + y * 8 + z


def coordinates():
    row, col = lax.axis_index("row"), lax.axis_index("col")
    return row % 4, (col // 2) % 4, row // 4, col // 8, col % 2


def device(x, y, z_lo, z_hi, core):
    return z_lo * 4 + x, z_hi * 8 + y * 2 + core


def exchange_kernel(update, ab, home, panel, swap_b, swap_a, product, sems):
    send, recv, back_send, back_recv = [sems.at[n] for n in range(4)]
    bar = pltpu.get_barrier_semaphore()
    x, y, z_lo, z_hi, core = coordinates()
    z = z_hi * 2 + z_lo
    mine = chip_of(x, y, z)
    row, col = lax.axis_index("row"), lax.axis_index("col")
    partner = device(x, y, z_lo, z_hi, 1 - core)
    straight = core == z_lo

    def home_target(s):
        to_x, to_y = (x + s // 32) % 4, (y + (s // 8) % 4) % 4
        return to_x, to_y, (z_hi + (s // 2) % 4) % 4, (core + s) % 2

    def greet(s, _):
        to_x, to_y, to_z, to_core = home_target(s)
        to = device(to_x, to_y, core, to_z, to_core)

        @pl.when(jnp.logical_not(jnp.logical_and(s == 0, straight)))
        def _():
            pl.semaphore_signal(bar, inc=1, device_id=to, device_id_type=MESH)

        return 0

    lax.fori_loop(0, CHIPS, greet, 0)

    @pl.when(jnp.logical_not(straight))
    def _():
        pl.semaphore_signal(bar, inc=1, device_id=partner, device_id_type=MESH)

    pl.semaphore_wait(bar, CHIPS)

    def spread(s, _):
        to_x, to_y, to_z = (x + s // 32) % 4, (y + (s // 8) % 4) % 4, (z + s) % 8
        channel = chip_of(to_x, to_y, to_z)

        @pl.when(jnp.logical_and(s == 0, straight))
        def _():
            pltpu.make_async_copy(ab.at[channel], panel.at[col, x], recv).start()

        @pl.when(jnp.logical_not(jnp.logical_and(s == 0, straight)))
        def _():
            pltpu.make_async_remote_copy(
                ab.at[channel],
                panel.at[col, x],
                send,
                recv,
                device_id=device(to_x, to_y, to_z % 2, to_z // 2, z_lo),
                device_id_type=MESH,
            ).start()

        return 0

    lax.fori_loop(0, CHIPS, spread, 0)
    pltpu.make_async_copy(panel, panel, recv).wait()

    def swap(source, target, at):
        return pltpu.make_async_remote_copy(
            source, target, sems.at[4 + at], sems.at[6 + at], device_id=partner, device_id_type=MESH
        )

    swaps = [swap(panel.at[:, :, 1], swap_b, 0)]
    if update == 1:
        swaps.append(swap(panel.at[pl.ds(16 * (1 - core), 16), :, 0], swap_a, 1))
    for copy in swaps:
        copy.start()
    for copy in swaps:
        copy.wait()

    if update == 0:
        left = jnp.concatenate([panel[:, n, 0].reshape(1024, 128) for n in range(4)], axis=1)
        for half, source in ((core, panel.at[:, :, 1]), (1 - core, swap_b)):
            right = jnp.concatenate([source[:, n].reshape(1024, 128) for n in range(4)], axis=1)
            out = lax.dot_general(
                right, left, (((0,), (0,)), ((), ())), preferred_element_type=jnp.float32
            ).astype(jnp.bfloat16)
            for n in range(4):
                product[pl.ds(16 * half, 16), n] = out[:, 128 * n : 128 * n + 128].reshape(16, 32, 128)
    else:
        own = pl.ds(16 * core, 16)
        left = jnp.concatenate(
            [panel[own, n, 0].reshape(512, 128) for n in range(4)]
            + [swap_a[:, n].reshape(512, 128) for n in range(4)],
            axis=1,
        )
        for half in range(2):
            part = slice(16 * half, 16 * half + 16)
            right = jnp.concatenate(
                [panel[part, n, 1].reshape(512, 128) for n in range(4)]
                + [swap_b[part, n].reshape(512, 128) for n in range(4)],
                axis=1,
            )
            out = lax.dot_general(
                right, left, (((1,), (1,)), ((), ())), preferred_element_type=jnp.float32
            ).astype(jnp.bfloat16)
            for n in range(4):
                product[part, n] = out[:, 128 * n : 128 * n + 128].reshape(16, 32, 128)

    def give_back(s, _):
        to_x, to_y, to_z, to_core = home_target(s)
        to = device(to_x, to_y, core, to_z, to_core)

        @pl.when(jnp.logical_and(s == 0, straight))
        def _():
            pltpu.make_async_copy(product.at[to[1], to_x], home.at[mine], back_recv).start()

        @pl.when(jnp.logical_not(jnp.logical_and(s == 0, straight)))
        def _():
            pltpu.make_async_remote_copy(
                product.at[to[1], to_x],
                home.at[mine],
                back_send,
                back_recv,
                device_id=to,
                device_id_type=MESH,
            ).start()

        return 0

    lax.fori_loop(0, CHIPS, give_back, 0)
    pltpu.make_async_copy(home, home, back_recv).wait()

    rest = ab.at[pl.ds(0, CHIPS - 1)], home.at[pl.ds(0, CHIPS - 1)]
    pltpu.make_async_copy(rest[0], rest[0], send).wait()
    pltpu.make_async_copy(rest[1], rest[1], back_send).wait()

    @pl.when(jnp.logical_not(straight))
    def _():
        pltpu.make_async_copy(ab.at[0], ab.at[0], send).wait()
        pltpu.make_async_copy(home.at[0], home.at[0], back_send).wait()


def exchange(ab, update):
    vmem = pl.BlockSpec(memory_space=pltpu.VMEM)
    return pl.pallas_call(
        functools.partial(exchange_kernel, update),
        out_shape=jax.ShapeDtypeStruct((CHIPS, 32, 128), jnp.bfloat16),
        in_specs=[vmem],
        out_specs=vmem,
        scratch_shapes=[
            pltpu.VMEM((32, 4, 2, 32, 128), jnp.bfloat16),
            pltpu.VMEM((32, 4, 32, 128), jnp.bfloat16),
            pltpu.VMEM((16, 4, 32, 128), jnp.bfloat16),
            pltpu.VMEM((32, 4, 32, 128), jnp.bfloat16),
            pltpu.SemaphoreType.DMA((8,)),
        ],
        compiler_params=pltpu.CompilerParams(
            collective_id=update, has_side_effects=True, vmem_limit_bytes=32 << 20
        ),
        name=f"exchange{update}",
    )(ab)


def layer_norm(values, gain, bias, axis):
    mean = jnp.mean(values, axis=axis, keepdims=True)
    var = jnp.mean(jnp.square(values - mean), axis=axis, keepdims=True)
    return (values - mean) * lax.rsqrt(var + EPS) * gain + bias


def triangle(block, index, in_gain, w_in, out_gain, out_bias, w_out, w_gate_out):
    hidden = w_out.shape[1]
    x = layer_norm(block.astype(jnp.float32), in_gain[index], 0.0, -1).astype(jnp.bfloat16)
    mixed = jnp.einsum("itc,cd->dti", x, w_in[index], preferred_element_type=jnp.float32)
    left = (mixed[0:hidden] * jax.nn.sigmoid(mixed[2 * hidden : 3 * hidden])).astype(jnp.bfloat16)
    right = (mixed[hidden : 2 * hidden] * jax.nn.sigmoid(mixed[3 * hidden : 4 * hidden])).astype(
        jnp.bfloat16
    )
    home = exchange(jnp.stack([left, right], axis=1), index).astype(jnp.float32)
    normed = layer_norm(
        home, out_gain[index][:, None, None], out_bias[index][:, None, None], 0
    ).astype(jnp.bfloat16)
    projected = jnp.einsum("dji,dc->ijc", normed, w_out[index], preferred_element_type=jnp.float32)
    gate = jnp.einsum("itc,cd->itd", x, w_gate_out[index], preferred_element_type=jnp.float32)
    return (block.astype(jnp.float32) + projected * jax.nn.sigmoid(gate)).astype(jnp.bfloat16)


def local(pair, in_gain, w_in, out_gain, out_bias, w_out, w_gate_out):
    first = triangle(pair, 0, in_gain, w_in, out_gain, out_bias, w_out, w_gate_out)
    return triangle(first, 1, in_gain, w_in, out_gain, out_bias, w_out, w_gate_out)


def solution(mesh):
    in_specs = (P("row", "col", None), P(), P(), P(), P(), P(), P())
    out_specs = P("row", "col", None)
    return jax.shard_map(local, mesh=mesh, in_specs=in_specs, out_specs=out_specs, check_vma=False)
```

```python
import jax
import jax.numpy as jnp
from jax import lax
from jax.experimental import pallas as pl
from jax.experimental.pallas import tpu as pltpu
from jax.sharding import PartitionSpec as P

EPS = 1e-05
MESH = pl.DeviceIdType.MESH
CHIPS = 128
BLOCKS = 8
WIDE = 512

F32, BF16 = jnp.float32, jnp.bfloat16


def coordinates():
    row, col = lax.axis_index("row"), lax.axis_index("col")
    return row % 4, (col // 2) % 4, row // 4, col // 8, col % 2


def device(x, y, z_lo, z_hi, core):
    return z_lo * 4 + x, z_hi * 8 + y * 2 + core


def sigmoid(values):
    return 0.5 * jnp.tanh(0.5 * values) + 0.5


def norm(values):
    mean = jnp.sum(values, axis=0, keepdims=True) * (1.0 / 128)
    centred = values - mean
    var = jnp.sum(centred * centred, axis=0, keepdims=True) * (1.0 / 128)
    return centred * lax.rsqrt(var + EPS)


def wide(column):
    return jnp.concatenate([column] * (WIDE // 128), axis=1)


def kernel(
    pair, in_gain, w_in, out_gain, out_bias, w_out, w_gate, updated,
    rows32, out_rows, z, x_all, gate, staged, total, gains, wt_in, wt_out, wt_gate,
    ab0, ab1, panel0, panel1, swap_b0, swap_b1, swap_a1, product0, product1, home0, home1,
    send_sems, recv_sems, swap_send, swap_recv, back_send, back_recv,
):
    bar = pltpu.get_barrier_semaphore()
    x, y, z_lo, z_hi, core = coordinates()
    z_at = z_hi * 2 + z_lo
    col = lax.axis_index("col")
    partner = device(x, y, z_lo, z_hi, 1 - core)
    straight = core == z_lo

    def home_target(s):
        to_x, to_y = (x + s // 32) % 4, (y + (s // 8) % 4) % 4
        return device(to_x, to_y, core, (z_hi + (s // 2) % 4) % 4, (core + s) % 2)

    def greet(s, _):
        @pl.when(jnp.logical_not(jnp.logical_and(s == 0, straight)))
        def _():
            pl.semaphore_signal(bar, inc=1, device_id=home_target(s), device_id_type=MESH)

        return 0

    lax.fori_loop(0, CHIPS, greet, 0)

    @pl.when(jnp.logical_not(straight))
    def _():
        pl.semaphore_signal(bar, inc=1, device_id=partner, device_id_type=MESH)

    def flip(block):
        return block.astype(F32).T

    def weights(u):
        for kind in range(4):
            turned = flip(w_in[u, :, 128 * kind : 128 * kind + 128]).astype(BF16)
            wt_in[u, :, kind] = turned.reshape(4, 32, 128)
        gains[3 * u] = jnp.broadcast_to(in_gain[u : u + 1, :], (128, 128)).T

    def late_weights(u):
        wt_out[u] = flip(w_out[u]).astype(BF16)
        wt_gate[u] = flip(w_gate[u]).astype(BF16)
        gains[3 * u + 1] = jnp.broadcast_to(out_gain[u : u + 1, :], (128, 128)).T
        gains[3 * u + 2] = jnp.broadcast_to(out_bias[u : u + 1, :], (128, 128)).T

    def take(t):
        return rows32[pl.ds(t, 128, stride=32), :]

    def projections(u, ab, group):
        lhs = wt_in[u, group].reshape(128, 128)

        def block(n, _):
            mixed = jnp.dot(lhs, x_all[n], preferred_element_type=F32)
            gated = mixed[0:64] * sigmoid(mixed[64:128])
            for kind in range(2):
                for q in range(4):
                    staged[pl.ds(kind * 32 + n * 4 + q, 32, stride=64), :] = gated[
                        32 * kind : 32 * kind + 32, 128 * q : 128 * q + 128
                    ]
            return 0

        lax.fori_loop(0, BLOCKS, block, 0)

        def pack(d, _):
            at = pl.multiple_of(d * 256, 256)
            ab[pl.ds(group * 32 + d * 4, 4)] = (
                staged[pl.ds(at, 256), :].astype(BF16).reshape(4, 2, 32, 128)
            )
            return 0

        lax.fori_loop(0, 8, pack, 0)

    def gates(u):
        def block(n, _):
            gate[n] = sigmoid(jnp.dot(wt_gate[u], x_all[n], preferred_element_type=F32))
            return 0

        lax.fori_loop(0, BLOCKS, block, 0)

    def forward(u, ab, panel):
        outer, inner = (y, x) if u == 0 else (x, y)
        slot = panel.at[y, z_hi * 2 + core, x] if u == 0 else panel.at[x, col]
        send, recv = send_sems.at[u], recv_sems.at[u, outer]
        for d in range(4):
            to_outer = (outer + d) % 4
            projections(u, ab, to_outer)
            if u == 0 and d == 0:
                pl.semaphore_wait(bar, CHIPS)

            def spread(s, _, d=d, to_outer=to_outer):
                to_inner, to_z = (inner + s // 8) % 4, (z_at + s) % 8
                channel = to_outer * 32 + to_inner * 8 + to_z
                to_x, to_y = (to_inner, to_outer) if u == 0 else (to_outer, to_inner)

                def remote():
                    pltpu.make_async_remote_copy(
                        ab.at[channel],
                        slot,
                        send,
                        recv,
                        device_id=device(to_x, to_y, to_z % 2, to_z // 2, z_lo),
                        device_id_type=MESH,
                    ).start()

                if d > 0:
                    remote()
                else:
                    own = jnp.logical_and(s == 0, straight)

                    @pl.when(own)
                    def _():
                        pltpu.make_async_copy(ab.at[channel], slot, recv).start()

                    @pl.when(jnp.logical_not(own))
                    def _():
                        remote()

                return 0

            lax.fori_loop(0, 32, spread, 0)

    def swap(u, chunk, source, target, at):
        return pltpu.make_async_remote_copy(
            source,
            target,
            swap_send.at[u, at, chunk],
            swap_recv.at[u, at, chunk],
            device_id=partner,
            device_id_type=MESH,
        )

    def lanes(parts):
        return jnp.concatenate(parts, axis=1)

    def multiply0(panel, swap_b, product):
        for d in range(4):
            at = (y + 4 - d) % 4
            pltpu.make_async_copy(panel.at[at], panel.at[at], recv_sems.at[0, at]).wait()
            copy = swap(0, at, panel.at[at, :, :, 1], swap_b.at[at], 0)
            copy.start()
            left = lanes([panel[at, :, n, 0].reshape(256, 128) for n in range(4)])
            for side in range(2):
                if side == 0:
                    right = lanes([panel[at, :, n, 1].reshape(256, 128) for n in range(4)])
                else:
                    copy.wait()
                    right = lanes([swap_b[at, :, n].reshape(256, 128) for n in range(4)])
                out = lax.dot_general(
                    right, left, (((0,), (0,)), ((), ())), preferred_element_type=F32
                )
                if d > 0:
                    out += total[side]
                if d < 3:
                    total[side] = out
                else:
                    half = core if side == 0 else 1 - core
                    done = out.astype(BF16)
                    for n in range(4):
                        product[pl.ds(16 * half, 16), n] = done[
                            :, 128 * n : 128 * n + 128
                        ].reshape(16, 32, 128)

    def multiply1(panel, swap_b, swap_a, product):
        for d in range(4):
            at = (x + 4 - d) % 4
            pltpu.make_async_copy(panel.at[at], panel.at[at], recv_sems.at[1, at]).wait()
            copies = [
                swap(1, at, panel.at[at, :, 1], swap_b.at[at], 0),
                swap(1, at, panel.at[at, pl.ds(16 * (1 - core), 16), 0], swap_a.at[at], 1),
            ]
            for copy in copies:
                copy.start()
            for copy in copies:
                copy.wait()
            left = lanes(
                [
                    panel[at, pl.ds(16 * core, 16), 0].reshape(512, 128),
                    swap_a[at].reshape(512, 128),
                ]
            )
            for side in range(2):
                part = slice(16 * side, 16 * side + 16)
                right = lanes(
                    [panel[at, part, 1].reshape(512, 128), swap_b[at, part].reshape(512, 128)]
                )
                out = lax.dot_general(
                    right, left, (((1,), (1,)), ((), ())), preferred_element_type=F32
                )
                if d > 0:
                    out += total[side]
                if d < 3:
                    total[side] = out
                else:
                    done = out.astype(BF16)
                    for n in range(4):
                        product[part, n] = done[:, 128 * n : 128 * n + 128].reshape(16, 32, 128)

    def give_back(u, product, home):
        channel = (y * 32 + x * 8 if u == 0 else x * 32 + y * 8) + z_at

        def one(s, _):
            to = home_target(s)
            block = product.at[to[1], to[0] % 4]
            own = jnp.logical_and(s == 0, straight)

            @pl.when(own)
            def _():
                pltpu.make_async_copy(block, home.at[channel], back_recv.at[u]).start()

            @pl.when(jnp.logical_not(own))
            def _():
                pltpu.make_async_remote_copy(
                    block,
                    home.at[channel],
                    back_send.at[u],
                    back_recv.at[u],
                    device_id=to,
                    device_id_type=MESH,
                ).start()

            return 0

        lax.fori_loop(0, CHIPS, one, 0)

    def to_rows(source):
        def part(n, _):
            at = pl.multiple_of(n * 512, 512)
            rows32[pl.ds(at, 512), :] = source[pl.ds(n * 16, 16)].reshape(512, 128).astype(F32)
            return 0

        lax.fori_loop(0, 8, part, 0)

    def finish(u, n):
        t = lanes([take(n * 4 + q) for q in range(4)])
        tn = norm(t) * wide(gains[3 * u + 1]) + wide(gains[3 * u + 2])
        projected = jnp.dot(wt_out[u], tn.astype(BF16), preferred_element_type=F32)
        return (z[n].astype(F32) + projected * gate[n]).astype(BF16)

    def enter(u, n, block):
        z[n] = block
        x_all[n] = (norm(block.astype(F32)) * wide(gains[3 * u])).astype(BF16)

    weights(0)
    to_rows(pair)

    def first(n, _):
        enter(0, n, lanes([take(n * 4 + q).T for q in range(4)]).astype(BF16))
        return 0

    lax.fori_loop(0, BLOCKS, first, 0)
    forward(0, ab0, panel0)
    late_weights(0)
    gates(0)
    weights(1)
    late_weights(1)
    multiply0(panel0, swap_b0, product0)
    give_back(0, product0, home0)
    pltpu.make_async_copy(home0, home0, back_recv.at[0]).wait()
    to_rows(home0)

    def second(n, _):
        enter(1, n, finish(0, n))
        return 0

    lax.fori_loop(0, BLOCKS, second, 0)
    forward(1, ab1, panel1)
    gates(1)
    multiply1(panel1, swap_b1, swap_a1, product1)
    give_back(1, product1, home1)
    pltpu.make_async_copy(home1, home1, back_recv.at[1]).wait()
    to_rows(home1)

    def last(n, _):
        block = finish(1, n).astype(F32)
        for q in range(4):
            out_rows[pl.ds(n * 4 + q, 128, stride=32), :] = block[:, 128 * q : 128 * q + 128].T
        return 0

    lax.fori_loop(0, BLOCKS, last, 0)

    def leave(n, _):
        at = pl.multiple_of(n * 512, 512)
        updated[pl.ds(n * 16, 16)] = out_rows[pl.ds(at, 512), :].astype(BF16).reshape(16, 32, 128)
        return 0

    lax.fori_loop(0, 8, leave, 0)

    for u, ab in ((0, ab0), (1, ab1)):
        rest = ab.at[pl.ds(0, CHIPS - 1)]
        pltpu.make_async_copy(rest, rest, send_sems.at[u]).wait()
        rest = home0.at[pl.ds(0, CHIPS - 1)]
        pltpu.make_async_copy(rest, rest, back_send.at[u]).wait()

        @pl.when(jnp.logical_not(straight))
        def _(u=u, ab=ab):
            pltpu.make_async_copy(ab.at[0], ab.at[0], send_sems.at[u]).wait()
            pltpu.make_async_copy(home0.at[0], home0.at[0], back_send.at[u]).wait()


def local(pair, in_gain, w_in, out_gain, out_bias, w_out, w_gate_out):
    vmem = pl.BlockSpec(memory_space=pltpu.VMEM)
    spread = pltpu.VMEM((CHIPS, 2, 32, 128), BF16)
    block = pltpu.VMEM((CHIPS, 32, 128), BF16)
    return pl.pallas_call(
        kernel,
        out_shape=jax.ShapeDtypeStruct(pair.shape, BF16),
        in_specs=[vmem] * 7,
        out_specs=vmem,
        scratch_shapes=[
            pltpu.VMEM((4096, 128), F32),
            pltpu.VMEM((4096, 128), F32),
            pltpu.VMEM((BLOCKS, 128, WIDE), BF16),
            pltpu.VMEM((BLOCKS, 128, WIDE), BF16),
            pltpu.VMEM((BLOCKS, 128, WIDE), F32),
            pltpu.VMEM((2048, 128), F32),
            pltpu.VMEM((2, 512, 512), F32),
            pltpu.VMEM((6, 128, 128), F32),
            pltpu.VMEM((2, 4, 4, 32, 128), BF16),
            pltpu.VMEM((2, 128, 128), BF16),
            pltpu.VMEM((2, 128, 128), BF16),
            spread,
            spread,
            pltpu.VMEM((4, 8, 4, 2, 32, 128), BF16),
            pltpu.VMEM((4, 32, 2, 32, 128), BF16),
            pltpu.VMEM((4, 8, 4, 32, 128), BF16),
            pltpu.VMEM((4, 32, 32, 128), BF16),
            pltpu.VMEM((4, 16, 32, 128), BF16),
            pltpu.VMEM((32, 4, 32, 128), BF16),
            pltpu.VMEM((32, 4, 32, 128), BF16),
            block,
            block,
            pltpu.SemaphoreType.DMA((2,)),
            pltpu.SemaphoreType.DMA((2, 4)),
            pltpu.SemaphoreType.DMA((2, 2, 4)),
            pltpu.SemaphoreType.DMA((2, 2, 4)),
            pltpu.SemaphoreType.DMA((2,)),
            pltpu.SemaphoreType.DMA((2,)),
        ],
        compiler_params=pltpu.CompilerParams(
            collective_id=0, has_side_effects=True, vmem_limit_bytes=56 << 20
        ),
        name="triangles",
    )(pair, in_gain, w_in, out_gain, out_bias, w_out, w_gate_out)


def solution(mesh):
    in_specs = (P("row", "col", None), P(), P(), P(), P(), P(), P())
    out_specs = P("row", "col", None)
    return jax.shard_map(local, mesh=mesh, in_specs=in_specs, out_specs=out_specs, check_vma=False)
```

```python
import jax
import jax.numpy as jnp
from jax import lax
from jax.experimental import pallas as pl
from jax.experimental.pallas import tpu as pltpu
from jax.sharding import PartitionSpec as P

EPS = 1e-05
MESH = pl.DeviceIdType.MESH
CHIPS = 128
BLOCKS = 8
WIDE = 512

F32, BF16 = jnp.float32, jnp.bfloat16


def coordinates():
    row, col = lax.axis_index("row"), lax.axis_index("col")
    return row % 4, (col // 2) % 4, row // 4, col // 8, col % 2


def device(x, y, z_lo, z_hi, core):
    return z_lo * 4 + x, z_hi * 8 + y * 2 + core


def sigmoid(values):
    return 0.5 * jnp.tanh(0.5 * values) + 0.5


def norm(values):
    mean = jnp.sum(values, axis=0, keepdims=True) * (1.0 / 128)
    centred = values - mean
    var = jnp.sum(centred * centred, axis=0, keepdims=True) * (1.0 / 128)
    return centred * lax.rsqrt(var + EPS)


def wide(column):
    return jnp.concatenate([column] * (WIDE // 128), axis=1)


def kernel(
    pair, in_gain, w_in, out_gain, out_bias, w_out, w_gate, updated,
    rows32, out_rows, z, x_all, gate, staged, total, gains, wt_in, wt_out, wt_gate,
    ab0, ab1, panel0, panel1, swap_b0, swap_b1, swap_a1, product0, product1, home0, home1,
    send_sems, recv_sems, swap_send, swap_recv, back_send, back_recv, line_sems,
):
    bar = pltpu.get_barrier_semaphore()
    x, y, z_lo, z_hi, core = coordinates()
    z_at = z_hi * 2 + z_lo
    col = lax.axis_index("col")
    partner = device(x, y, z_lo, z_hi, 1 - core)
    straight = core == z_lo

    def home_target(s):
        to_x, to_y = (x + s // 32) % 4, (y + (s // 8) % 4) % 4
        return device(to_x, to_y, core, (z_hi + (s // 2) % 4) % 4, (core + s) % 2)

    along_z = [
        device(x, y, (z_at + d) % 8 % 2, (z_at + d) % 8 // 2, other)
        for d in range(8)
        for other in (core, 1 - core)
    ][1:]
    along_y = [device(x, (y + d) % 4, z_lo, z_hi, core) for d in range(1, 4)]
    along_x = [device((x + d) % 4, y, z_lo, z_hi, core) for d in range(1, 4)]

    def greet(sem, devices):
        for to in devices:
            pl.semaphore_signal(sem, inc=1, device_id=to, device_id_type=MESH)

    greet(bar, along_z + along_y + along_x)

    def flip(block):
        return block.astype(F32).T

    def weights(u):
        for kind in range(4):
            turned = flip(w_in[u, :, 128 * kind : 128 * kind + 128]).astype(BF16)
            wt_in[u, :, kind] = turned.reshape(4, 32, 128)
        gains[3 * u] = jnp.broadcast_to(in_gain[u : u + 1, :], (128, 128)).T

    def late_weights(u):
        wt_out[u] = flip(w_out[u]).astype(BF16)
        wt_gate[u] = flip(w_gate[u]).astype(BF16)
        gains[3 * u + 1] = jnp.broadcast_to(out_gain[u : u + 1, :], (128, 128)).T
        gains[3 * u + 2] = jnp.broadcast_to(out_bias[u : u + 1, :], (128, 128)).T

    def take(t):
        return rows32[pl.ds(t, 128, stride=32), :]

    def projections(u, ab, group):
        lhs = wt_in[u, group].reshape(128, 128)

        def block(n, _):
            mixed = jnp.dot(lhs, x_all[n], preferred_element_type=F32)
            gated = mixed[0:64] * sigmoid(mixed[64:128])
            for kind in range(2):
                for q in range(4):
                    staged[pl.ds(kind * 32 + n * 4 + q, 32, stride=64), :] = gated[
                        32 * kind : 32 * kind + 32, 128 * q : 128 * q + 128
                    ]
            return 0

        lax.fori_loop(0, BLOCKS, block, 0)

        def pack(d, _):
            at = pl.multiple_of(d * 256, 256)
            ab[pl.ds(group * 32 + d * 4, 4)] = (
                staged[pl.ds(at, 256), :].astype(BF16).reshape(4, 2, 32, 128)
            )
            return 0

        lax.fori_loop(0, 8, pack, 0)

    def gates(u):
        def block(n, _):
            gate[n] = sigmoid(jnp.dot(wt_gate[u], x_all[n], preferred_element_type=F32))
            return 0

        lax.fori_loop(0, BLOCKS, block, 0)

    def forward(u, ab, panel):
        outer, inner = (y, x) if u == 0 else (x, y)
        slot = panel.at[y, z_hi * 2 + core, x] if u == 0 else panel.at[x, col]
        send, recv = send_sems.at[u], recv_sems.at[u, outer]
        for d in range(4):
            to_outer = (outer + d) % 4
            projections(u, ab, to_outer)
            if u == 0 and d == 0:
                pl.semaphore_wait(line_sems.at[1], 3)

            def spread(s, _, d=d, to_outer=to_outer):
                to_inner, to_z = (inner + s // 8) % 4, (z_at + s) % 8
                channel = to_outer * 32 + to_inner * 8 + to_z
                to_x, to_y = (to_inner, to_outer) if u == 0 else (to_outer, to_inner)

                def remote():
                    pltpu.make_async_remote_copy(
                        ab.at[channel],
                        slot,
                        send,
                        recv,
                        device_id=device(to_x, to_y, to_z % 2, to_z // 2, z_lo),
                        device_id_type=MESH,
                    ).start()

                if d > 0:
                    remote()
                else:
                    own = jnp.logical_and(s == 0, straight)

                    @pl.when(own)
                    def _():
                        pltpu.make_async_copy(ab.at[channel], slot, recv).start()

                    @pl.when(jnp.logical_not(own))
                    def _():
                        remote()

                return 0

            lax.fori_loop(0, 32, spread, 0)

    def swap(u, chunk, source, target, at):
        return pltpu.make_async_remote_copy(
            source,
            target,
            swap_send.at[u, at, chunk],
            swap_recv.at[u, at, chunk],
            device_id=partner,
            device_id_type=MESH,
        )

    def lanes(parts):
        return jnp.concatenate(parts, axis=1)

    def multiply0(panel, swap_b, product):
        for d in range(4):
            at = (y + 4 - d) % 4
            pltpu.make_async_copy(panel.at[at], panel.at[at], recv_sems.at[0, at]).wait()
            copy = swap(0, at, panel.at[at, :, :, 1], swap_b.at[at], 0)
            copy.start()
            left = lanes([panel[at, :, n, 0].reshape(256, 128) for n in range(4)])
            for side in range(2):
                if side == 0:
                    right = lanes([panel[at, :, n, 1].reshape(256, 128) for n in range(4)])
                else:
                    copy.wait()
                    right = lanes([swap_b[at, :, n].reshape(256, 128) for n in range(4)])
                out = lax.dot_general(
                    right, left, (((0,), (0,)), ((), ())), preferred_element_type=F32
                )
                if d > 0:
                    out += total[side]
                if d < 3:
                    total[side] = out
                else:
                    half = core if side == 0 else 1 - core
                    done = out.astype(BF16)
                    for n in range(4):
                        product[pl.ds(16 * half, 16), n] = done[
                            :, 128 * n : 128 * n + 128
                        ].reshape(16, 32, 128)

    def multiply1(panel, swap_b, swap_a, product):
        for d in range(4):
            at = (x + 4 - d) % 4
            pltpu.make_async_copy(panel.at[at], panel.at[at], recv_sems.at[1, at]).wait()
            copies = [
                swap(1, at, panel.at[at, :, 1], swap_b.at[at], 0),
                swap(1, at, panel.at[at, pl.ds(16 * (1 - core), 16), 0], swap_a.at[at], 1),
            ]
            for copy in copies:
                copy.start()
            for copy in copies:
                copy.wait()
            left = lanes(
                [
                    panel[at, pl.ds(16 * core, 16), 0].reshape(512, 128),
                    swap_a[at].reshape(512, 128),
                ]
            )
            for side in range(2):
                part = slice(16 * side, 16 * side + 16)
                right = lanes(
                    [panel[at, part, 1].reshape(512, 128), swap_b[at, part].reshape(512, 128)]
                )
                out = lax.dot_general(
                    right, left, (((1,), (1,)), ((), ())), preferred_element_type=F32
                )
                if d > 0:
                    out += total[side]
                if d < 3:
                    total[side] = out
                else:
                    done = out.astype(BF16)
                    for n in range(4):
                        product[part, n] = done[:, 128 * n : 128 * n + 128].reshape(16, 32, 128)

    def give_back(u, product, home):
        channel = (y * 32 + x * 8 if u == 0 else x * 32 + y * 8) + z_at

        def one(s, _):
            to = home_target(s)
            block = product.at[to[1], to[0] % 4]
            own = jnp.logical_and(s == 0, straight)

            @pl.when(own)
            def _():
                pltpu.make_async_copy(block, home.at[channel], back_recv.at[u]).start()

            @pl.when(jnp.logical_not(own))
            def _():
                pltpu.make_async_remote_copy(
                    block,
                    home.at[channel],
                    back_send.at[u],
                    back_recv.at[u],
                    device_id=to,
                    device_id_type=MESH,
                ).start()

            return 0

        lax.fori_loop(0, CHIPS, one, 0)

    def to_rows(source):
        def part(n, _):
            at = pl.multiple_of(n * 512, 512)
            rows32[pl.ds(at, 512), :] = source[pl.ds(n * 16, 16)].reshape(512, 128).astype(F32)
            return 0

        lax.fori_loop(0, 8, part, 0)

    def finish(u, n):
        t = lanes([take(n * 4 + q) for q in range(4)])
        tn = norm(t) * wide(gains[3 * u + 1]) + wide(gains[3 * u + 2])
        projected = jnp.dot(wt_out[u], tn.astype(BF16), preferred_element_type=F32)
        return (z[n].astype(F32) + projected * gate[n]).astype(BF16)

    def enter(u, n, block):
        z[n] = block
        x_all[n] = (norm(block.astype(F32)) * wide(gains[3 * u])).astype(BF16)

    weights(0)
    to_rows(pair)

    def first(n, _):
        enter(0, n, lanes([take(n * 4 + q).T for q in range(4)]).astype(BF16))
        return 0

    pl.semaphore_wait(bar, 21)
    greet(line_sems.at[0], along_y)
    lax.fori_loop(0, 4, first, 0)
    pl.semaphore_wait(line_sems.at[0], 3)
    greet(line_sems.at[1], along_x)
    lax.fori_loop(4, BLOCKS, first, 0)
    forward(0, ab0, panel0)
    late_weights(0)
    gates(0)
    weights(1)
    late_weights(1)
    multiply0(panel0, swap_b0, product0)
    give_back(0, product0, home0)
    pltpu.make_async_copy(home0, home0, back_recv.at[0]).wait()
    to_rows(home0)

    def second(n, _):
        enter(1, n, finish(0, n))
        return 0

    lax.fori_loop(0, BLOCKS, second, 0)
    forward(1, ab1, panel1)
    gates(1)
    multiply1(panel1, swap_b1, swap_a1, product1)
    give_back(1, product1, home1)
    pltpu.make_async_copy(home1, home1, back_recv.at[1]).wait()
    to_rows(home1)

    def last(n, _):
        block = finish(1, n).astype(F32)
        for q in range(4):
            out_rows[pl.ds(n * 4 + q, 128, stride=32), :] = block[:, 128 * q : 128 * q + 128].T
        return 0

    lax.fori_loop(0, BLOCKS, last, 0)

    def leave(n, _):
        at = pl.multiple_of(n * 512, 512)
        updated[pl.ds(n * 16, 16)] = out_rows[pl.ds(at, 512), :].astype(BF16).reshape(16, 32, 128)
        return 0

    lax.fori_loop(0, 8, leave, 0)

    for u, ab in ((0, ab0), (1, ab1)):
        rest = ab.at[pl.ds(0, CHIPS - 1)]
        pltpu.make_async_copy(rest, rest, send_sems.at[u]).wait()
        rest = home0.at[pl.ds(0, CHIPS - 1)]
        pltpu.make_async_copy(rest, rest, back_send.at[u]).wait()

        @pl.when(jnp.logical_not(straight))
        def _(u=u, ab=ab):
            pltpu.make_async_copy(ab.at[0], ab.at[0], send_sems.at[u]).wait()
            pltpu.make_async_copy(home0.at[0], home0.at[0], back_send.at[u]).wait()


def local(pair, in_gain, w_in, out_gain, out_bias, w_out, w_gate_out):
    vmem = pl.BlockSpec(memory_space=pltpu.VMEM)
    spread = pltpu.VMEM((CHIPS, 2, 32, 128), BF16)
    block = pltpu.VMEM((CHIPS, 32, 128), BF16)
    return pl.pallas_call(
        kernel,
        out_shape=jax.ShapeDtypeStruct(pair.shape, BF16),
        in_specs=[vmem] * 7,
        out_specs=vmem,
        scratch_shapes=[
            pltpu.VMEM((4096, 128), F32),
            pltpu.VMEM((4096, 128), F32),
            pltpu.VMEM((BLOCKS, 128, WIDE), BF16),
            pltpu.VMEM((BLOCKS, 128, WIDE), BF16),
            pltpu.VMEM((BLOCKS, 128, WIDE), F32),
            pltpu.VMEM((2048, 128), F32),
            pltpu.VMEM((2, 512, 512), F32),
            pltpu.VMEM((6, 128, 128), F32),
            pltpu.VMEM((2, 4, 4, 32, 128), BF16),
            pltpu.VMEM((2, 128, 128), BF16),
            pltpu.VMEM((2, 128, 128), BF16),
            spread,
            spread,
            pltpu.VMEM((4, 8, 4, 2, 32, 128), BF16),
            pltpu.VMEM((4, 32, 2, 32, 128), BF16),
            pltpu.VMEM((4, 8, 4, 32, 128), BF16),
            pltpu.VMEM((4, 32, 32, 128), BF16),
            pltpu.VMEM((4, 16, 32, 128), BF16),
            pltpu.VMEM((32, 4, 32, 128), BF16),
            pltpu.VMEM((32, 4, 32, 128), BF16),
            block,
            block,
            pltpu.SemaphoreType.DMA((2,)),
            pltpu.SemaphoreType.DMA((2, 4)),
            pltpu.SemaphoreType.DMA((2, 2, 4)),
            pltpu.SemaphoreType.DMA((2, 2, 4)),
            pltpu.SemaphoreType.DMA((2,)),
            pltpu.SemaphoreType.DMA((2,)),
            pltpu.SemaphoreType.REGULAR((2,)),
        ],
        compiler_params=pltpu.CompilerParams(
            collective_id=0, has_side_effects=True, vmem_limit_bytes=56 << 20
        ),
        name="triangles",
    )(pair, in_gain, w_in, out_gain, out_bias, w_out, w_gate_out)


def solution(mesh):
    in_specs = (P("row", "col", None), P(), P(), P(), P(), P(), P())
    out_specs = P("row", "col", None)
    return jax.shard_map(local, mesh=mesh, in_specs=in_specs, out_specs=out_specs, check_vma=False)
```

```python
import jax
import jax.numpy as jnp
from jax import lax
from jax.experimental import pallas as pl
from jax.experimental.pallas import tpu as pltpu
from jax.sharding import PartitionSpec as P

EPS = 1e-05
MESH = pl.DeviceIdType.MESH
CHIPS = 128
BLOCKS = 8
WIDE = 512

F32, BF16 = jnp.float32, jnp.bfloat16


def coordinates():
    row, col = lax.axis_index("row"), lax.axis_index("col")
    return row % 4, (col // 2) % 4, row // 4, col // 8, col % 2


def device(x, y, z_lo, z_hi, core):
    return z_lo * 4 + x, z_hi * 8 + y * 2 + core


def sigmoid(values):
    return 0.5 * jnp.tanh(0.5 * values) + 0.5


def norm(values):
    mean = jnp.sum(values, axis=0, keepdims=True) * (1.0 / 128)
    centred = values - mean
    var = jnp.sum(centred * centred, axis=0, keepdims=True) * (1.0 / 128)
    return centred * lax.rsqrt(var + EPS)


def wide(column):
    return jnp.concatenate([column] * (WIDE // 128), axis=1)


def kernel(
    pair, in_gain, w_in, out_gain, out_bias, w_out, w_gate, updated,
    pair_v, out_v, rows, out_rows, z, x_all, gate, staged, total, gains, wt_in, wt_out, wt_gate,
    ab0, ab1, panel0, panel1, swap_b0, swap_b1, swap_a1, product0, product1, home0, home1,
    send_sems, recv_sems, swap_send, swap_recv, back_send, back_recv, line_sem, local_sems,
):
    bar = pltpu.get_barrier_semaphore()
    x, y, z_lo, z_hi, core = coordinates()
    z_at = z_hi * 2 + z_lo
    col = lax.axis_index("col")
    partner = device(x, y, z_lo, z_hi, 1 - core)
    straight = core == z_lo
    parity = (x + y) % 2

    along_y = [device(x, (y + d) % 4, z_lo, z_hi, core) for d in range(1, 4)]

    def greet(sem, to):
        pl.semaphore_signal(sem, inc=1, device_id=to, device_id_type=MESH)

    def greet_plane(s, _):
        @pl.when(jnp.logical_not(jnp.logical_and(s == 0, straight)))
        def _():
            greet(bar, device((x + s // 8) % 4, y, core, (z_hi + s // 2) % 4, (core + s) % 2))

        return 0

    lax.fori_loop(0, 32, greet_plane, 0)
    for to in along_y:
        greet(bar, to)

    @pl.when(jnp.logical_not(straight))
    def _():
        greet(bar, partner)

    def half_of(ref, h):
        return ref.at[:, pl.ds(16 * h, 16)]

    arrivals = [
        pltpu.make_async_copy(half_of(pair, h), half_of(pair_v, h), local_sems.at[h])
        for h in range(2)
    ]
    for copy in arrivals:
        copy.start()

    def flip(block):
        return block.astype(F32).T

    def weights(u):
        for kind in range(4):
            turned = flip(w_in[u, :, 128 * kind : 128 * kind + 128]).astype(BF16)
            wt_in[u, :, kind] = turned.reshape(4, 32, 128)
        gains[3 * u] = jnp.broadcast_to(in_gain[u : u + 1, :], (128, 128)).T

    def late_weights(u):
        wt_out[u] = flip(w_out[u]).astype(BF16)
        wt_gate[u] = flip(w_gate[u]).astype(BF16)
        gains[3 * u + 1] = jnp.broadcast_to(out_gain[u : u + 1, :], (128, 128)).T
        gains[3 * u + 2] = jnp.broadcast_to(out_bias[u : u + 1, :], (128, 128)).T

    def take(t):
        return rows[pl.ds(t, 128, stride=16), :]

    def to_rows(source):
        def part(n, _):
            at = pl.multiple_of(n * 512, 512)
            rows[pl.ds(at, 512), :] = source[pl.ds(n * 32, 32)].reshape(512, 128).astype(F32)
            return 0

        lax.fori_loop(0, 4, part, 0)

    def projections(u, h, ab, group):
        lhs = wt_in[u, group].reshape(128, 128)

        def block(n, _):
            mixed = jnp.dot(lhs, x_all[4 * h + n], preferred_element_type=F32)
            gated = mixed[0:64] * sigmoid(mixed[64:128])
            for kind in range(2):
                for q in range(4):
                    staged[pl.ds(kind * 16 + n * 4 + q, 32, stride=32), :] = gated[
                        32 * kind : 32 * kind + 32, 128 * q : 128 * q + 128
                    ]
            return 0

        lax.fori_loop(0, 4, block, 0)

        def pack(d, _):
            at = pl.multiple_of(d * 256, 256)
            ab[h, pl.ds(group * 32 + d * 8, 8)] = (
                staged[pl.ds(at, 256), :].astype(BF16).reshape(8, 2, 16, 128)
            )
            return 0

        lax.fori_loop(0, 4, pack, 0)

    def gates(u):
        def block(n, _):
            gate[n] = sigmoid(jnp.dot(wt_gate[u], x_all[n], preferred_element_type=F32))
            return 0

        lax.fori_loop(0, BLOCKS, block, 0)

    def near(at):
        return [at, at + 1 - 2 * (at % 2), (at + 2) % 4, 3 - at]

    def forward(u, h, ab, panel):
        outer, inner = (y, x) if u == 0 else (x, y)
        slot = panel.at[y, z_hi * 2 + core, x, h] if u == 0 else panel.at[x, col, h]
        send, recv = send_sems.at[u], recv_sems.at[u, h, outer]
        for side in range(2):
            for e in range(4):
                to_outer = near(outer)[e]
                if e % 2 == 0:
                    projections(u, h, ab, side * 2 + to_outer // 2)
                if u == 0 and h == 0 and side == 0 and e == 0:
                    pl.semaphore_wait(bar, 35)
                    for to in along_y:
                        greet(line_sem, to)
                if u == 0 and h == 0 and side == 0 and e == 1:
                    pl.semaphore_wait(line_sem, 3)

                def spread(s, _, to_outer=to_outer, side=side, e=e):
                    odd = (side + to_outer) % 2
                    to_inner = odd + 2 * ((inner // 2 + s // 8) % 2)
                    to_z = (z_at + s) % 8
                    channel = side * 64 + to_outer * 16 + (to_inner // 2) * 8 + to_z
                    to_x, to_y = (to_inner, to_outer) if u == 0 else (to_outer, to_inner)

                    def remote():
                        pltpu.make_async_remote_copy(
                            ab.at[h, channel],
                            slot,
                            send,
                            recv,
                            device_id=device(to_x, to_y, to_z % 2, to_z // 2, z_lo),
                            device_id_type=MESH,
                        ).start()

                    if e > 0:
                        remote()
                    else:
                        own = jnp.logical_and(jnp.logical_and(s == 0, parity == side), straight)

                        @pl.when(own)
                        def _():
                            pltpu.make_async_copy(ab.at[h, channel], slot, recv).start()

                        @pl.when(jnp.logical_not(own))
                        def _():
                            remote()

                    return 0

                lax.fori_loop(0, 16, spread, 0)

    def swap(u, chunk, source, target, at):
        return pltpu.make_async_remote_copy(
            source,
            target,
            swap_send.at[u, at, chunk],
            swap_recv.at[u, at, chunk],
            device_id=partner,
            device_id_type=MESH,
        )

    def lanes(parts):
        return jnp.concatenate(parts, axis=1)

    def keep(product, part, out):
        done = out.astype(BF16)
        for n in range(4):
            product[part, n] = done[:, 128 * n : 128 * n + 128].reshape(16, 2, 16, 128)

    def multiply0(panel, swap_b, product):
        for d, at in enumerate(near(y)):
            for h in range(2):
                part = panel.at[at, :, :, h]
                pltpu.make_async_copy(part, part, recv_sems.at[0, h, at]).wait()
            copy = swap(0, at, panel.at[at, :, :, :, 1], swap_b.at[at], 0)
            copy.start()
            left = lanes([panel[at, :, n, :, 0].reshape(256, 128) for n in range(4)])
            for side in range(2):
                if side == 0:
                    right = lanes([panel[at, :, n, :, 1].reshape(256, 128) for n in range(4)])
                else:
                    copy.wait()
                    right = lanes([swap_b[at, :, n].reshape(256, 128) for n in range(4)])
                out = lax.dot_general(
                    right, left, (((0,), (0,)), ((), ())), preferred_element_type=F32
                )
                if d > 0:
                    out += total[side]
                if d < 3:
                    total[side] = out
                else:
                    keep(product, pl.ds(16 * (core if side == 0 else 1 - core), 16), out)

    def multiply1(panel, swap_b, swap_a, product):
        for d, at in enumerate(near(x)):
            for h in range(2):
                part = panel.at[at, :, h]
                pltpu.make_async_copy(part, part, recv_sems.at[1, h, at]).wait()
            copies = [
                swap(1, at, panel.at[at, :, :, 1], swap_b.at[at], 0),
                swap(1, at, panel.at[at, pl.ds(16 * (1 - core), 16), :, 0], swap_a.at[at], 1),
            ]
            for copy in copies:
                copy.start()
            for copy in copies:
                copy.wait()
            left = lanes(
                [
                    panel[at, pl.ds(16 * core, 16), :, 0].reshape(512, 128),
                    swap_a[at].reshape(512, 128),
                ]
            )
            for side in range(2):
                part = slice(16 * side, 16 * side + 16)
                right = lanes(
                    [panel[at, part, :, 1].reshape(512, 128), swap_b[at, part].reshape(512, 128)]
                )
                out = lax.dot_general(
                    right, left, (((1,), (1,)), ((), ())), preferred_element_type=F32
                )
                if d > 0:
                    out += total[side]
                if d < 3:
                    total[side] = out
                else:
                    keep(product, part, out)

    def home_target(s):
        to_x, to_y = (x + s // 32) % 4, (y + (s // 8) % 4) % 4
        return device(to_x, to_y, core, (z_hi + (s // 2) % 4) % 4, (core + s) % 2)

    def give_back(u, product, home):
        outer, inner = (y, x) if u == 0 else (x, y)
        channel = parity * 64 + outer * 16 + (inner // 2) * 8 + z_at
        for h in range(2):

            def one(s, _, h=h):
                to = home_target(s)
                block, slot = product.at[to[1], to[0] % 4, h], home.at[h, channel]
                own = jnp.logical_and(s == 0, straight)

                @pl.when(own)
                def _():
                    pltpu.make_async_copy(block, slot, back_recv.at[u, h]).start()

                @pl.when(jnp.logical_not(own))
                def _():
                    pltpu.make_async_remote_copy(
                        block,
                        slot,
                        back_send.at[u],
                        back_recv.at[u, h],
                        device_id=to,
                        device_id_type=MESH,
                    ).start()

                return 0

            lax.fori_loop(0, CHIPS, one, 0)

    def received(u, h, home):
        pltpu.make_async_copy(home.at[h], home.at[h], back_recv.at[u, h]).wait()
        to_rows(home.at[h])

    def finish(u, h, n):
        t = lanes([take(n * 4 + q) for q in range(4)])
        tn = norm(t) * wide(gains[3 * u + 1]) + wide(gains[3 * u + 2])
        projected = jnp.dot(wt_out[u], tn.astype(BF16), preferred_element_type=F32)
        return (z[4 * h + n].astype(F32) + projected * gate[4 * h + n]).astype(BF16)

    def enter(u, h, n, block):
        z[4 * h + n] = block
        x_all[4 * h + n] = (norm(block.astype(F32)) * wide(gains[3 * u])).astype(BF16)

    weights(0)
    for h in range(2):
        arrivals[h].wait()
        to_rows(half_of(pair_v, h))

        def first(n, _, h=h):
            enter(0, h, n, lanes([take(n * 4 + q).T for q in range(4)]).astype(BF16))
            return 0

        lax.fori_loop(0, 4, first, 0)
        forward(0, h, ab0, panel0)
    late_weights(0)
    gates(0)
    weights(1)
    late_weights(1)
    multiply0(panel0, swap_b0, product0)
    give_back(0, product0, home0)
    for h in range(2):
        received(0, h, home0)

        def second(n, _, h=h):
            enter(1, h, n, finish(0, h, n))
            return 0

        lax.fori_loop(0, 4, second, 0)
        forward(1, h, ab1, panel1)
    gates(1)
    multiply1(panel1, swap_b1, swap_a1, product1)
    give_back(1, product1, home1)
    leaving = []
    for h in range(2):
        received(1, h, home1)

        def last(n, _, h=h):
            block = finish(1, h, n).astype(F32)
            for q in range(4):
                staged_out = block[:, 128 * q : 128 * q + 128].T
                out_rows[pl.ds(n * 4 + q, 128, stride=16), :] = staged_out
            return 0

        lax.fori_loop(0, 4, last, 0)

        def leave(n, _, h=h):
            at = pl.multiple_of(n * 512, 512)
            out_v[pl.ds(n * 32, 32), 16 * h : 16 * h + 16] = (
                out_rows[pl.ds(at, 512), :].astype(BF16).reshape(32, 16, 128)
            )
            return 0

        lax.fori_loop(0, 4, leave, 0)
        copy = pltpu.make_async_copy(half_of(out_v, h), half_of(updated, h), local_sems.at[2 + h])
        copy.start()
        leaving.append(copy)

    for u, ab in ((0, ab0), (1, ab1)):
        for sent, sem in ((ab, send_sems.at[u]), (home0, back_send.at[u])):
            rest = sent.at[:, pl.ds(0, CHIPS - 1)]
            pltpu.make_async_copy(rest, rest, sem).wait()

            @pl.when(jnp.logical_not(straight))
            def _(sent=sent, sem=sem):
                rest = sent.at[:, 0]
                pltpu.make_async_copy(rest, rest, sem).wait()

    for copy in leaving:
        copy.wait()


def local(pair, in_gain, w_in, out_gain, out_bias, w_out, w_gate_out):
    vmem = pl.BlockSpec(memory_space=pltpu.VMEM)
    anywhere = pl.BlockSpec(memory_space=pl.ANY)
    spread = pltpu.VMEM((2, CHIPS, 2, 16, 128), BF16)
    block = pltpu.VMEM((2, CHIPS, 16, 128), BF16)
    whole = pltpu.VMEM((128, 32, 128), BF16)
    return pl.pallas_call(
        kernel,
        out_shape=jax.ShapeDtypeStruct(pair.shape, BF16),
        in_specs=[anywhere] + [vmem] * 6,
        out_specs=anywhere,
        scratch_shapes=[
            whole,
            whole,
            pltpu.VMEM((2048, 128), F32),
            pltpu.VMEM((2048, 128), F32),
            pltpu.VMEM((BLOCKS, 128, WIDE), BF16),
            pltpu.VMEM((BLOCKS, 128, WIDE), BF16),
            pltpu.VMEM((BLOCKS, 128, WIDE), F32),
            pltpu.VMEM((1024, 128), F32),
            pltpu.VMEM((2, 512, 512), F32),
            pltpu.VMEM((6, 128, 128), F32),
            pltpu.VMEM((2, 4, 4, 32, 128), BF16),
            pltpu.VMEM((2, 128, 128), BF16),
            pltpu.VMEM((2, 128, 128), BF16),
            spread,
            spread,
            pltpu.VMEM((4, 8, 4, 2, 2, 16, 128), BF16),
            pltpu.VMEM((4, 32, 2, 2, 16, 128), BF16),
            pltpu.VMEM((4, 8, 4, 2, 16, 128), BF16),
            pltpu.VMEM((4, 32, 2, 16, 128), BF16),
            pltpu.VMEM((4, 16, 2, 16, 128), BF16),
            pltpu.VMEM((32, 4, 2, 16, 128), BF16),
            pltpu.VMEM((32, 4, 2, 16, 128), BF16),
            block,
            block,
            pltpu.SemaphoreType.DMA((2,)),
            pltpu.SemaphoreType.DMA((2, 2, 4)),
            pltpu.SemaphoreType.DMA((2, 2, 4)),
            pltpu.SemaphoreType.DMA((2, 2, 4)),
            pltpu.SemaphoreType.DMA((2,)),
            pltpu.SemaphoreType.DMA((2, 2)),
            pltpu.SemaphoreType.REGULAR,
            pltpu.SemaphoreType.DMA((4,)),
        ],
        compiler_params=pltpu.CompilerParams(
            collective_id=0, has_side_effects=True, vmem_limit_bytes=56 << 20
        ),
        name="triangles",
    )(pair, in_gain, w_in, out_gain, out_bias, w_out, w_gate_out)


def solution(mesh):
    in_specs = (P("row", "col", None), P(), P(), P(), P(), P(), P())
    out_specs = P("row", "col", None)
    return jax.shard_map(local, mesh=mesh, in_specs=in_specs, out_specs=out_specs, check_vma=False)
```

```python
import jax
import jax.numpy as jnp
from jax import lax
from jax.experimental import pallas as pl
from jax.experimental.pallas import tpu as pltpu
from jax.sharding import PartitionSpec as P

EPS = 1e-05
MESH = pl.DeviceIdType.MESH
CHIPS = 128
BLOCKS = 8
WIDE = 512

F32, BF16 = jnp.float32, jnp.bfloat16


def coordinates():
    row, col = lax.axis_index("row"), lax.axis_index("col")
    return row % 4, (col // 2) % 4, row // 4, col // 8, col % 2


def device(x, y, z_lo, z_hi, core):
    return z_lo * 4 + x, z_hi * 8 + y * 2 + core


def sigmoid(values):
    return 0.5 * jnp.tanh(0.5 * values) + 0.5


def norm(values):
    mean = jnp.sum(values, axis=0, keepdims=True) * (1.0 / 128)
    centred = values - mean
    var = jnp.sum(centred * centred, axis=0, keepdims=True) * (1.0 / 128)
    return centred * lax.rsqrt(var + EPS)


def wide(column):
    return jnp.concatenate([column] * (WIDE // 128), axis=1)


def kernel(
    pair, in_gain, w_in, out_gain, out_bias, w_out, w_gate, updated,
    pair_v, out_v, rows, out_rows, z, x_all, gate, staged, gains, wt_in, wt_out, wt_gate,
    ab0, ab1, panel0, panel1, swap_b0, swap_b1, swap_a1, product0, product1, home0, home1,
    send_sems, recv_sems, swap_send, swap_recv, back_send, back_recv, line_sems, local_sems,
):
    bar = pltpu.get_barrier_semaphore()
    x, y, z_lo, z_hi, core = coordinates()
    z_at = z_hi * 2 + z_lo
    col = lax.axis_index("col")
    partner = device(x, y, z_lo, z_hi, 1 - core)
    straight = core == z_lo

    along_y = [device(x, (y + d) % 4, z_lo, z_hi, core) for d in range(1, 4)]
    along_x = [device((x + d) % 4, y, z_lo, z_hi, core) for d in range(1, 4)]

    def greet(sem, devices):
        for to in devices:
            pl.semaphore_signal(sem, inc=1, device_id=to, device_id_type=MESH)

    column = [device(x, y, core, (z_hi + n // 2) % 4, (core + n) % 2) for n in range(8)]
    greet(bar, column[1:])

    @pl.when(straight)
    def _():
        greet(bar, along_y + along_x)

    @pl.when(jnp.logical_not(straight))
    def _():
        greet(bar, along_y + along_x + [column[0], partner])

    def half_of(ref, h):
        return ref.at[:, pl.ds(16 * h, 16)]

    arrival = pltpu.make_async_copy(pair, pair_v, local_sems.at[0])
    arrival.start()

    def flip(block):
        return block.astype(F32).T

    def weights(u):
        for kind in range(4):
            turned = flip(w_in[u, :, 128 * kind : 128 * kind + 128]).astype(BF16)
            wt_in[u, :, kind] = turned.reshape(4, 32, 128)
        gains[3 * u] = jnp.broadcast_to(in_gain[u : u + 1, :], (128, 128)).T

    def late_weights(u):
        wt_out[u] = flip(w_out[u]).astype(BF16)
        wt_gate[u] = flip(w_gate[u]).astype(BF16)
        gains[3 * u + 1] = jnp.broadcast_to(out_gain[u : u + 1, :], (128, 128)).T
        gains[3 * u + 2] = jnp.broadcast_to(out_bias[u : u + 1, :], (128, 128)).T

    def take(t, tokens):
        return rows[pl.ds(t, 128, stride=tokens), :]

    def to_rows(source):
        tokens = source.shape[1]
        some = 512 // tokens

        def part(n, _):
            at = pl.multiple_of(n * 512, 512)
            rows[pl.ds(at, 512), :] = source[pl.ds(n * some, some)].reshape(512, 128).astype(F32)
            return 0

        lax.fori_loop(0, 128 // some, part, 0)

    def projections(u, h, ab, group):
        lhs = wt_in[u, group].reshape(128, 128)
        tokens = ab.shape[2]

        def block(n, _):
            mixed = jnp.dot(lhs, x_all[4 * h + n], preferred_element_type=F32)
            gated = mixed[0:64] * sigmoid(mixed[64:128])
            for kind in range(2):
                for q in range(4):
                    staged[pl.ds(kind * tokens + n * 4 + q, 32, stride=2 * tokens), :] = gated[
                        32 * kind : 32 * kind + 32, 128 * q : 128 * q + 128
                    ]
            return 0

        lax.fori_loop(0, tokens // 4, block, 0)
        some = 128 // tokens

        def pack(d, _):
            at = pl.multiple_of(d * 256, 256)
            ab[pl.ds(group * 32 + d * some, some)] = (
                staged[pl.ds(at, 256), :].astype(BF16).reshape(some, 2, tokens, 128)
            )
            return 0

        lax.fori_loop(0, 32 // some, pack, 0)

    def gates(u):
        def block(n, _):
            gate[n] = sigmoid(jnp.dot(wt_gate[u], x_all[n], preferred_element_type=F32))
            return 0

        lax.fori_loop(0, BLOCKS, block, 0)

    def near(u):
        if u == 0:
            return [(x + d) % 4 for d in (0, 2, 1, 3)]
        return [y, y + 1 - 2 * (y % 2), (y + 2) % 4, 3 - y]

    def forward(u, h, ab, slot, recv):
        inner = y if u == 0 else x
        send = send_sems.at[u]
        for e, to_outer in enumerate(near(u)):
            projections(u, h, ab, to_outer)
            if u == 0 and e == 0:
                pl.semaphore_wait(bar, 14)
                greet(line_sems.at[0], along_y)
            if u == 0 and e == 1:
                pl.semaphore_wait(line_sems.at[1], 3)

            def spread(s, _, to_outer=to_outer, e=e):
                to_inner, to_z = (inner + s // 8) % 4, (z_at + s) % 8
                channel = to_outer * 32 + to_inner * 8 + to_z
                to_x, to_y = (to_outer, to_inner) if u == 0 else (to_inner, to_outer)

                def remote():
                    pltpu.make_async_remote_copy(
                        ab.at[channel],
                        slot,
                        send,
                        recv,
                        device_id=device(to_x, to_y, to_z % 2, to_z // 2, z_lo),
                        device_id_type=MESH,
                    ).start()

                if e > 0:
                    remote()
                else:
                    own = jnp.logical_and(s == 0, straight)

                    @pl.when(own)
                    def _():
                        pltpu.make_async_copy(ab.at[channel], slot, recv).start()

                    @pl.when(jnp.logical_not(own))
                    def _():
                        remote()

                return 0

            if u == 0 and e == 0:
                lax.fori_loop(0, 8, spread, 0)
                pl.semaphore_wait(line_sems.at[0], 3)
                greet(line_sems.at[1], along_x)
                lax.fori_loop(8, 32, spread, 0)
            else:
                lax.fori_loop(0, 32, spread, 0)

    def swap(u, chunk, source, target, at):
        return pltpu.make_async_remote_copy(
            source,
            target,
            swap_send.at[u, at, chunk],
            swap_recv.at[u, at, chunk],
            device_id=partner,
            device_id_type=MESH,
        )

    def lanes(parts):
        return jnp.concatenate(parts, axis=1)

    def product_of(right, left, over):
        return lax.dot_general(
            right, left, (((over,), (over,)), ((), ())), preferred_element_type=F32
        ).astype(BF16)

    def multiply0(panel, swap_b, product, home):
        def left(p):
            return lanes([panel[p + 2 * n, :, 0].reshape(1024, 128) for n in range(2)])

        def right(p, side):
            if side == 0:
                return lanes([panel[p + 2 * n, :, 1].reshape(1024, 128) for n in range(2)])
            return lanes([swap_b[p + 2 * n].reshape(1024, 128) for n in range(2)])

        def part(p, q, side):
            out = product_of(right(p, side), left(q), 0)
            half = core if side == 0 else 1 - core
            for n in range(2):
                for m in range(2):
                    product[pl.ds(16 * half + 4 * (p + 2 * n), 4), q + 2 * m] = out[
                        128 * n : 128 * n + 128, 128 * m : 128 * m + 128
                    ].reshape(4, 2, 16, 128)

        def arrive(at):
            pltpu.make_async_copy(panel.at[at], panel.at[at], recv_sems.at[at]).wait()
            copy = swap(0, at, panel.at[at, :, 1], swap_b.at[at], 0)
            copy.start()
            return copy

        p = x % 2
        order = near(0)
        copies = [arrive(at) for at in order[:2]]
        part(p, p, 0)
        for copy in copies:
            copy.wait()
        part(p, p, 1)
        give_back(0, p, product, home, ((0, 0),), (0, 1))
        copies = [arrive(at) for at in order[2:]]
        for side in range(2):
            if side == 1:
                for copy in copies:
                    copy.wait()
            part(p, 1 - p, side)
            part(1 - p, p, side)
            part(1 - p, 1 - p, side)
        for h in range(2):
            give_back(0, p, product, home, ((0, 1), (1, 0), (1, 1)), (h,))

    def multiply1(panel, swap_b, swap_a, product, home):
        def left(p):
            def some(source, start):
                return jnp.concatenate(
                    [
                        source(2 * p + m, pl.ds(start + 2 * n, 2)).reshape(64, 128)
                        for n in range(2)
                        for m in range(2)
                    ],
                    axis=0,
                )

            return lanes(
                [some(lambda at, zc: panel[at, zc, n, :, 0], 4 * core) for n in range(4)]
                + [some(lambda at, zc: swap_a[at, zc, n], 0) for n in range(4)]
            )

        def right(at):
            return lanes(
                [panel[at, :, n, :, 1].reshape(256, 128) for n in range(4)]
                + [swap_b[at, :, n].reshape(256, 128) for n in range(4)]
            )

        def part(p, q):
            for m in range(2):
                out = product_of(right(2 * p + m), left(q), 1)
                for n in range(2):
                    product[2 * p + m, :, 2 * n + q] = out[:, 128 * n : 128 * n + 128].reshape(
                        8, 2, 16, 128
                    )

        def arrive(at):
            for h in range(2):
                block = panel.at[at, :, :, h]
                pltpu.make_async_copy(block, block, recv_sems.at[4 + 4 * h + at]).wait()
            copies = [
                swap(1, at, panel.at[at, :, :, :, 1], swap_b.at[at], 0),
                swap(1, at, panel.at[at, pl.ds(4 * (1 - core), 4), :, :, 0], swap_a.at[at], 1),
            ]
            for copy in copies:
                copy.start()
            return copies

        p = y // 2
        order = near(1)
        for copy in arrive(order[0]) + arrive(order[1]):
            copy.wait()
        part(p, p)
        give_back(1, p, product, home, ((0, 0),), (0, 1))
        for copy in arrive(order[2]) + arrive(order[3]):
            copy.wait()
        part(p, 1 - p)
        part(1 - p, p)
        part(1 - p, 1 - p)
        for h in range(2):
            give_back(1, p, product, home, ((0, 1), (1, 0), (1, 1)), (h,))

    def give_back(u, p, product, home, quarters, halves):
        channel = (x * 32 + y * 8 if u == 0 else y * 32 + x * 8) + z_at
        for h in halves:
            for of_x, of_y in quarters:

                def one(s, _, h=h, of_x=of_x, of_y=of_y):
                    to_x = (p + of_x) % 2 + 2 * ((x // 2 + s // 16) % 2)
                    to_y = 2 * ((p + of_y) % 2) + (y + s // 8) % 2
                    to_z, to_core = (z_hi + s // 2) % 4, (core + s) % 2
                    to = device(to_x, to_y, core, to_z, to_core)
                    if u == 0:
                        block = product.at[to[1], to_x, h]
                    else:
                        block = product.at[to_y, to_z * 2 + to_core, to_x, h]
                    slot = home.at[h, channel]
                    here = jnp.logical_and(to_x == x, to_y == y)
                    own = jnp.logical_and(jnp.logical_and(s % 8 == 0, straight), here)

                    @pl.when(own)
                    def _():
                        pltpu.make_async_copy(block, slot, back_recv.at[u, h]).start()

                    @pl.when(jnp.logical_not(own))
                    def _():
                        pltpu.make_async_remote_copy(
                            block,
                            slot,
                            back_send.at[u],
                            back_recv.at[u, h],
                            device_id=to,
                            device_id_type=MESH,
                        ).start()

                    return 0

                lax.fori_loop(0, 32, one, 0)

    def received(u, h, home):
        pltpu.make_async_copy(home.at[h], home.at[h], back_recv.at[u, h]).wait()
        to_rows(home.at[h])

    def finish(u, h, n):
        t = lanes([take(n * 4 + q, 16) for q in range(4)])
        tn = norm(t) * wide(gains[3 * u + 1]) + wide(gains[3 * u + 2])
        projected = jnp.dot(wt_out[u], tn.astype(BF16), preferred_element_type=F32)
        return (z[4 * h + n].astype(F32) + projected * gate[4 * h + n]).astype(BF16)

    def enter(u, h, n, block):
        z[4 * h + n] = block
        x_all[4 * h + n] = (norm(block.astype(F32)) * wide(gains[3 * u])).astype(BF16)

    weights(0)
    arrival.wait()
    to_rows(pair_v)

    def first(n, _):
        enter(0, 0, n, lanes([take(n * 4 + q, 32).T for q in range(4)]).astype(BF16))
        return 0

    lax.fori_loop(0, BLOCKS, first, 0)
    forward(0, 0, ab0, panel0.at[x, col], recv_sems.at[x])
    late_weights(0)
    gates(0)
    weights(1)
    late_weights(1)
    multiply0(panel0, swap_b0, product0, home0)
    for h in range(2):
        received(0, h, home0)

        def second(n, _, h=h):
            enter(1, h, n, finish(0, h, n))
            return 0

        lax.fori_loop(0, 4, second, 0)
        slot = panel1.at[y, z_hi * 2 + core, x, h]
        forward(1, h, ab1.at[h], slot, recv_sems.at[4 + 4 * h + y])
    gates(1)
    multiply1(panel1, swap_b1, swap_a1, product1, home1)
    leaving = []
    for h in range(2):
        received(1, h, home1)

        def last(n, _, h=h):
            block = finish(1, h, n).astype(F32)
            for q in range(4):
                staged_out = block[:, 128 * q : 128 * q + 128].T
                out_rows[pl.ds(n * 4 + q, 128, stride=16), :] = staged_out
            return 0

        lax.fori_loop(0, 4, last, 0)

        def leave(n, _, h=h):
            at = pl.multiple_of(n * 512, 512)
            out_v[pl.ds(n * 32, 32), 16 * h : 16 * h + 16] = (
                out_rows[pl.ds(at, 512), :].astype(BF16).reshape(32, 16, 128)
            )
            return 0

        lax.fori_loop(0, 4, leave, 0)
        copy = pltpu.make_async_copy(half_of(out_v, h), half_of(updated, h), local_sems.at[1 + h])
        copy.start()
        leaving.append(copy)

    for sent, sem in (
        (ab0, send_sems.at[0]),
        (ab1, send_sems.at[1]),
        (home0, back_send.at[0]),
        (home1, back_send.at[1]),
    ):
        chips = () if sent is ab0 else (slice(None),)
        rest = sent.at[(*chips, pl.ds(0, CHIPS - 1))]
        pltpu.make_async_copy(rest, rest, sem).wait()

        @pl.when(jnp.logical_not(straight))
        def _(sent=sent, sem=sem, chips=chips):
            rest = sent.at[(*chips, 0)]
            pltpu.make_async_copy(rest, rest, sem).wait()

    for copy in leaving:
        copy.wait()


def local(pair, in_gain, w_in, out_gain, out_bias, w_out, w_gate_out):
    vmem = pl.BlockSpec(memory_space=pltpu.VMEM)
    anywhere = pl.BlockSpec(memory_space=pl.ANY)
    block = pltpu.VMEM((2, CHIPS, 16, 128), BF16)
    whole = pltpu.VMEM((128, 32, 128), BF16)
    return pl.pallas_call(
        kernel,
        out_shape=jax.ShapeDtypeStruct(pair.shape, BF16),
        in_specs=[anywhere] + [vmem] * 6,
        out_specs=anywhere,
        scratch_shapes=[
            whole,
            whole,
            pltpu.VMEM((4096, 128), F32),
            pltpu.VMEM((2048, 128), F32),
            pltpu.VMEM((BLOCKS, 128, WIDE), BF16),
            pltpu.VMEM((BLOCKS, 128, WIDE), BF16),
            pltpu.VMEM((BLOCKS, 128, WIDE), F32),
            pltpu.VMEM((2048, 128), F32),
            pltpu.VMEM((6, 128, 128), F32),
            pltpu.VMEM((2, 4, 4, 32, 128), BF16),
            pltpu.VMEM((2, 128, 128), BF16),
            pltpu.VMEM((2, 128, 128), BF16),
            pltpu.VMEM((CHIPS, 2, 32, 128), BF16),
            pltpu.VMEM((2, CHIPS, 2, 16, 128), BF16),
            pltpu.VMEM((4, 32, 2, 32, 128), BF16),
            pltpu.VMEM((4, 8, 4, 2, 2, 16, 128), BF16),
            pltpu.VMEM((4, 32, 32, 128), BF16),
            pltpu.VMEM((4, 8, 4, 2, 16, 128), BF16),
            pltpu.VMEM((4, 4, 4, 2, 16, 128), BF16),
            pltpu.VMEM((32, 4, 2, 16, 128), BF16),
            pltpu.VMEM((4, 8, 4, 2, 16, 128), BF16),
            block,
            block,
            pltpu.SemaphoreType.DMA((2,)),
            pltpu.SemaphoreType.DMA((12,)),
            pltpu.SemaphoreType.DMA((2, 2, 4)),
            pltpu.SemaphoreType.DMA((2, 2, 4)),
            pltpu.SemaphoreType.DMA((2,)),
            pltpu.SemaphoreType.DMA((2, 2)),
            pltpu.SemaphoreType.REGULAR((2,)),
            pltpu.SemaphoreType.DMA((3,)),
        ],
        compiler_params=pltpu.CompilerParams(
            collective_id=0, has_side_effects=True, vmem_limit_bytes=56 << 20
        ),
        name="triangles",
    )(pair, in_gain, w_in, out_gain, out_bias, w_out, w_gate_out)


def solution(mesh):
    in_specs = (P("row", "col", None), P(), P(), P(), P(), P(), P())
    out_specs = P("row", "col", None)
    return jax.shard_map(local, mesh=mesh, in_specs=in_specs, out_specs=out_specs, check_vma=False)
```

```python
import jax
import jax.numpy as jnp
from jax import lax
from jax.experimental import pallas as pl
from jax.experimental.pallas import tpu as pltpu
from jax.sharding import PartitionSpec as P

EPS = 1e-05
MESH = pl.DeviceIdType.MESH
CHIPS = 128
BLOCKS = 8
WIDE = 512

F32, BF16 = jnp.float32, jnp.bfloat16


def coordinates():
    row, col = lax.axis_index("row"), lax.axis_index("col")
    return row % 4, (col // 2) % 4, row // 4, col // 8, col % 2


def device(x, y, z_lo, z_hi, core):
    return z_lo * 4 + x, z_hi * 8 + y * 2 + core


def rem(value, by):
    return lax.rem(value, jnp.int32(by))


def div(value, by):
    return lax.div(value, jnp.int32(by))


def sigmoid(values):
    return 0.5 * jnp.tanh(0.5 * values) + 0.5


def norm(values):
    mean = jnp.sum(values, axis=0, keepdims=True) * (1.0 / 128)
    centred = values - mean
    var = jnp.sum(centred * centred, axis=0, keepdims=True) * (1.0 / 128)
    return centred * lax.rsqrt(var + EPS)


def wide(column):
    return jnp.concatenate([column] * (WIDE // 128), axis=1)


def kernel(
    pair, in_gain_hbm, w_in_hbm, out_gain_hbm, out_bias_hbm, w_out_hbm, w_gate_hbm, updated,
    in_gain, w_in, out_gain, out_bias, w_out, w_gate, pair_v, out_v, rows, out_rows, z, x_all, gate, staged, gains, wt_in, wt_out, wt_gate,
    ab0, ab1, panel0, panel1, swap_b0, swap_b1, swap_a1, product0, product1, home0, home1,
    send_sems, recv_sems, swap_send, swap_recv, back_send, back_recv, line_sems, local_sems,
):
    bar = pltpu.get_barrier_semaphore()
    x, y, z_lo, z_hi, core = coordinates()
    z_at = z_hi * 2 + z_lo
    col = lax.axis_index("col")
    partner = device(x, y, z_lo, z_hi, 1 - core)
    straight = core == z_lo

    along_y = [device(x, (y + d) % 4, z_lo, z_hi, core) for d in range(1, 4)]
    along_x = [device((x + d) % 4, y, z_lo, z_hi, core) for d in range(1, 4)]

    def greet(sem, devices):
        for to in devices:
            pl.semaphore_signal(sem, inc=1, device_id=to, device_id_type=MESH)

    column = [device(x, y, core, (z_hi + n // 2) % 4, (core + n) % 2) for n in range(8)]
    greet(bar, column[1:])

    @pl.when(straight)
    def _():
        greet(bar, along_y + along_x)

    @pl.when(jnp.logical_not(straight))
    def _():
        greet(bar, along_y + along_x + [column[0], partner])

    def half_of(ref, h):
        return ref.at[:, pl.ds(16 * h, 16)]

    arrivals = [
        pltpu.make_async_copy(source, target, local_sems.at[n])
        for n, (source, target) in enumerate(
            (
                (pair, pair_v),
                (w_in_hbm, w_in),
                (in_gain_hbm, in_gain),
                (out_gain_hbm, out_gain),
                (out_bias_hbm, out_bias),
                (w_out_hbm, w_out),
                (w_gate_hbm, w_gate),
            )
        )
    ]
    for copy in arrivals:
        copy.start()

    def flip(block):
        return block.astype(F32).T

    def weights(u):
        for kind in range(4):
            turned = flip(w_in[u, :, 128 * kind : 128 * kind + 128]).astype(BF16)
            wt_in[u, :, kind] = turned.reshape(4, 32, 128)
        gains[3 * u] = jnp.broadcast_to(in_gain[u : u + 1, :], (128, 128)).T

    def late_weights(u):
        wt_out[u] = flip(w_out[u]).astype(BF16)
        wt_gate[u] = flip(w_gate[u]).astype(BF16)
        gains[3 * u + 1] = jnp.broadcast_to(out_gain[u : u + 1, :], (128, 128)).T
        gains[3 * u + 2] = jnp.broadcast_to(out_bias[u : u + 1, :], (128, 128)).T

    def take(t, tokens):
        return rows[pl.ds(t, 128, stride=tokens), :]

    def to_rows(source):
        tokens = source.shape[1]
        some = 512 // tokens

        def part(n, _):
            at = pl.multiple_of(n * 512, 512)
            rows[pl.ds(at, 512), :] = source[pl.ds(n * some, some)].reshape(512, 128).astype(F32)
            return 0

        lax.fori_loop(0, 128 // some, part, 0)

    def projections(u, h, ab, group):
        lhs = wt_in[u, group].reshape(128, 128)
        tokens = ab.shape[2]

        def block(n, _):
            mixed = jnp.dot(lhs, x_all[4 * h + n], preferred_element_type=F32)
            gated = mixed[0:64] * sigmoid(mixed[64:128])
            for kind in range(2):
                for q in range(4):
                    staged[pl.ds(kind * tokens + n * 4 + q, 32, stride=2 * tokens), :] = gated[
                        32 * kind : 32 * kind + 32, 128 * q : 128 * q + 128
                    ]
            return 0

        lax.fori_loop(0, tokens // 4, block, 0)
        some = 128 // tokens

        def pack(d, _):
            at = pl.multiple_of(d * 256, 256)
            ab[pl.ds(group * 32 + d * some, some)] = (
                staged[pl.ds(at, 256), :].astype(BF16).reshape(some, 2, tokens, 128)
            )
            return 0

        lax.fori_loop(0, 32 // some, pack, 0)

    def gates(u):
        def block(n, _):
            gate[n] = sigmoid(jnp.dot(wt_gate[u], x_all[n], preferred_element_type=F32))
            return 0

        lax.fori_loop(0, BLOCKS, block, 0)

    def near(u):
        if u == 0:
            return [(x + d) % 4 for d in (0, 2, 1, 3)]
        return [y, y + 1 - 2 * (y % 2), (y + 2) % 4, 3 - y]

    def forward(u, h, ab, slot, recv):
        inner = y if u == 0 else x
        send = send_sems.at[u]
        for e, to_outer in enumerate(near(u)):
            projections(u, h, ab, to_outer)
            if u == 0 and e == 0:
                pl.semaphore_wait(bar, 14)
                greet(line_sems.at[0], along_y)
            if u == 0 and e == 1:
                pl.semaphore_wait(line_sems.at[1], 3)

            def spread(s, _, to_outer=to_outer, e=e):
                to_inner, to_z = rem(inner + div(s, 8), 4), rem(z_at + 3 * s, 8)
                channel = to_outer * 32 + to_inner * 8 + to_z
                to_x, to_y = (to_outer, to_inner) if u == 0 else (to_inner, to_outer)

                def remote():
                    pltpu.make_async_remote_copy(
                        ab.at[channel],
                        slot,
                        send,
                        recv,
                        device_id=device(to_x, to_y, rem(to_z, 2), div(to_z, 2), z_lo),
                        device_id_type=MESH,
                    ).start()

                if e > 0:
                    remote()
                else:
                    own = jnp.logical_and(s == 0, straight)

                    @pl.when(own)
                    def _():
                        pltpu.make_async_copy(ab.at[channel], slot, recv).start()

                    @pl.when(jnp.logical_not(own))
                    def _():
                        remote()

                return 0

            if u == 0 and e == 0:
                lax.fori_loop(0, 8, spread, 0)
                pl.semaphore_wait(line_sems.at[0], 3)
                greet(line_sems.at[1], along_x)
                lax.fori_loop(8, 32, spread, 0)
            else:
                lax.fori_loop(0, 32, spread, 0)

    def swap(u, chunk, source, target, at):
        return pltpu.make_async_remote_copy(
            source,
            target,
            swap_send.at[u, at, chunk],
            swap_recv.at[u, at, chunk],
            device_id=partner,
            device_id_type=MESH,
        )

    def lanes(parts):
        return jnp.concatenate(parts, axis=1)

    def product_of(right, left, over):
        return lax.dot_general(
            right, left, (((over,), (over,)), ((), ())), preferred_element_type=F32
        ).astype(BF16)

    def multiply0(panel, swap_b, product, home):
        def left(p):
            return lanes([panel[p + 2 * n, :, 0].reshape(1024, 128) for n in range(2)])

        def right(p, side):
            if side == 0:
                return lanes([panel[p + 2 * n, :, 1].reshape(1024, 128) for n in range(2)])
            return lanes([swap_b[p + 2 * n].reshape(1024, 128) for n in range(2)])

        def part(p, q, side):
            out = product_of(right(p, side), left(q), 0)
            half = core if side == 0 else 1 - core
            for n in range(2):
                for m in range(2):
                    product[pl.ds(16 * half + 4 * (p + 2 * n), 4), q + 2 * m] = out[
                        128 * n : 128 * n + 128, 128 * m : 128 * m + 128
                    ].reshape(4, 2, 16, 128)

        def arrive(at):
            pltpu.make_async_copy(panel.at[at], panel.at[at], recv_sems.at[at]).wait()
            copy = swap(0, at, panel.at[at, :, 1], swap_b.at[at], 0)
            copy.start()
            return copy

        p = x % 2
        order = near(0)
        copies = [arrive(at) for at in order[:2]]
        part(p, p, 0)
        for copy in copies:
            copy.wait()
        part(p, p, 1)
        give_back(0, p, product, home, ((0, 0),), (0, 1))
        copies = [arrive(at) for at in order[2:]]
        part(p, 1 - p, 0)
        part(p, 1 - p, 1)
        give_back(0, p, product, home, ((1, 0),), (0,))
        part(1 - p, p, 0)
        part(1 - p, 1 - p, 0)
        for copy in copies:
            copy.wait()
        part(1 - p, p, 1)
        give_back(0, p, product, home, ((0, 1),), (0,))
        part(1 - p, 1 - p, 1)
        give_back(0, p, product, home, ((1, 1),), (0,))
        give_back(0, p, product, home, ((1, 0), (0, 1), (1, 1)), (1,))

    def multiply1(panel, swap_b, swap_a, product, home):
        def left(p):
            def some(source, start):
                return jnp.concatenate(
                    [
                        source(2 * p + m, pl.ds(start + 2 * n, 2)).reshape(64, 128)
                        for n in range(2)
                        for m in range(2)
                    ],
                    axis=0,
                )

            return lanes(
                [some(lambda at, zc: panel[at, zc, n, :, 0], 4 * core) for n in range(4)]
                + [some(lambda at, zc: swap_a[at, zc, n], 0) for n in range(4)]
            )

        def right(at):
            return lanes(
                [panel[at, :, n, :, 1].reshape(256, 128) for n in range(4)]
                + [swap_b[at, :, n].reshape(256, 128) for n in range(4)]
            )

        def part(p, q):
            for m in range(2):
                out = product_of(right(2 * p + m), left(q), 1)
                for n in range(2):
                    product[2 * p + m, :, 2 * n + q] = out[:, 128 * n : 128 * n + 128].reshape(
                        8, 2, 16, 128
                    )

        def arrive(at):
            for h in range(2):
                block = panel.at[at, :, :, h]
                pltpu.make_async_copy(block, block, recv_sems.at[4 + 4 * h + at]).wait()
            copies = [
                swap(1, at, panel.at[at, :, :, :, 1], swap_b.at[at], 0),
                swap(1, at, panel.at[at, pl.ds(4 * (1 - core), 4), :, :, 0], swap_a.at[at], 1),
            ]
            for copy in copies:
                copy.start()
            return copies

        p = y // 2
        order = near(1)
        for copy in arrive(order[0]) + arrive(order[1]):
            copy.wait()
        part(p, p)
        give_back(1, p, product, home, ((0, 0),), (0, 1))
        for copy in arrive(order[2]) + arrive(order[3]):
            copy.wait()
        part(p, 1 - p)
        give_back(1, p, product, home, ((1, 0),), (0,))
        part(1 - p, p)
        give_back(1, p, product, home, ((0, 1),), (0,))
        part(1 - p, 1 - p)
        give_back(1, p, product, home, ((1, 1),), (0,))
        give_back(1, p, product, home, ((1, 0), (0, 1), (1, 1)), (1,))

    def give_back(u, p, product, home, quarters, halves):
        channel = (x * 32 + y * 8 if u == 0 else y * 32 + x * 8) + z_at
        for h in halves:
            for of_x, of_y in quarters:

                def one(s, _, h=h, of_x=of_x, of_y=of_y):
                    to_x = (p + of_x) % 2 + 2 * rem(x // 2 + div(s, 16), 2)
                    to_y = 2 * ((p + of_y) % 2) + rem(y + div(s, 8), 2)
                    to_z, to_core = rem(z_hi + div(s, 2), 4), rem(core + s, 2)
                    to = device(to_x, to_y, core, to_z, to_core)
                    if u == 0:
                        block = product.at[to[1], to_x, h]
                    else:
                        block = product.at[to_y, to_z * 2 + to_core, to_x, h]
                    slot = home.at[h, channel]
                    here = jnp.logical_and(to_x == x, to_y == y)
                    own = jnp.logical_and(jnp.logical_and(rem(s, 8) == 0, straight), here)

                    @pl.when(own)
                    def _():
                        pltpu.make_async_copy(block, slot, back_recv.at[u, h]).start()

                    @pl.when(jnp.logical_not(own))
                    def _():
                        pltpu.make_async_remote_copy(
                            block,
                            slot,
                            back_send.at[u],
                            back_recv.at[u, h],
                            device_id=to,
                            device_id_type=MESH,
                        ).start()

                    return 0

                lax.fori_loop(0, 32, one, 0)

    def received(u, h, home):
        pltpu.make_async_copy(home.at[h], home.at[h], back_recv.at[u, h]).wait()
        to_rows(home.at[h])

    def finish(u, h, n):
        t = lanes([take(n * 4 + q, 16) for q in range(4)])
        tn = norm(t) * wide(gains[3 * u + 1]) + wide(gains[3 * u + 2])
        projected = jnp.dot(wt_out[u], tn.astype(BF16), preferred_element_type=F32)
        return (z[4 * h + n].astype(F32) + projected * gate[4 * h + n]).astype(BF16)

    def enter(u, h, n, block):
        z[4 * h + n] = block
        x_all[4 * h + n] = (norm(block.astype(F32)) * wide(gains[3 * u])).astype(BF16)

    for copy in arrivals[:3]:
        copy.wait()
    weights(0)
    to_rows(pair_v)

    def first(n, _):
        enter(0, 0, n, lanes([take(n * 4 + q, 32).T for q in range(4)]).astype(BF16))
        return 0

    lax.fori_loop(0, BLOCKS, first, 0)
    forward(0, 0, ab0, panel0.at[x, col], recv_sems.at[x])
    for copy in arrivals[3:]:
        copy.wait()
    late_weights(0)
    gates(0)
    weights(1)
    late_weights(1)
    multiply0(panel0, swap_b0, product0, home0)
    for h in range(2):
        received(0, h, home0)

        def second(n, _, h=h):
            enter(1, h, n, finish(0, h, n))
            return 0

        lax.fori_loop(0, 4, second, 0)
        slot = panel1.at[y, z_hi * 2 + core, x, h]
        forward(1, h, ab1.at[h], slot, recv_sems.at[4 + 4 * h + y])
    gates(1)
    multiply1(panel1, swap_b1, swap_a1, product1, home1)
    leaving = []
    for h in range(2):
        received(1, h, home1)

        def last(n, _, h=h):
            block = finish(1, h, n).astype(F32)
            for q in range(4):
                staged_out = block[:, 128 * q : 128 * q + 128].T
                out_rows[pl.ds(n * 4 + q, 128, stride=16), :] = staged_out
            return 0

        lax.fori_loop(0, 4, last, 0)

        def leave(n, _, h=h):
            at = pl.multiple_of(n * 512, 512)
            out_v[pl.ds(n * 32, 32), 16 * h : 16 * h + 16] = (
                out_rows[pl.ds(at, 512), :].astype(BF16).reshape(32, 16, 128)
            )
            return 0

        lax.fori_loop(0, 4, leave, 0)
        copy = pltpu.make_async_copy(half_of(out_v, h), half_of(updated, h), local_sems.at[7 + h])
        copy.start()
        leaving.append(copy)

    for sent, sem in (
        (ab0, send_sems.at[0]),
        (ab1, send_sems.at[1]),
        (home0, back_send.at[0]),
        (home1, back_send.at[1]),
    ):
        chips = () if sent is ab0 else (slice(None),)
        rest = sent.at[(*chips, pl.ds(0, CHIPS - 1))]
        pltpu.make_async_copy(rest, rest, sem).wait()

        @pl.when(jnp.logical_not(straight))
        def _(sent=sent, sem=sem, chips=chips):
            rest = sent.at[(*chips, 0)]
            pltpu.make_async_copy(rest, rest, sem).wait()

    for copy in leaving:
        copy.wait()


def local(pair, in_gain, w_in, out_gain, out_bias, w_out, w_gate_out):
    anywhere = pl.BlockSpec(memory_space=pl.ANY)
    block = pltpu.VMEM((2, CHIPS, 16, 128), BF16)
    whole = pltpu.VMEM((128, 32, 128), BF16)
    return pl.pallas_call(
        kernel,
        out_shape=jax.ShapeDtypeStruct(pair.shape, BF16),
        in_specs=[anywhere] * 7,
        out_specs=anywhere,
        scratch_shapes=[
            pltpu.VMEM((2, 128), F32),
            pltpu.VMEM((2, 128, 512), BF16),
            pltpu.VMEM((2, 128), F32),
            pltpu.VMEM((2, 128), F32),
            pltpu.VMEM((2, 128, 128), BF16),
            pltpu.VMEM((2, 128, 128), BF16),
            whole,
            whole,
            pltpu.VMEM((4096, 128), F32),
            pltpu.VMEM((2048, 128), F32),
            pltpu.VMEM((BLOCKS, 128, WIDE), BF16),
            pltpu.VMEM((BLOCKS, 128, WIDE), BF16),
            pltpu.VMEM((BLOCKS, 128, WIDE), F32),
            pltpu.VMEM((2048, 128), F32),
            pltpu.VMEM((6, 128, 128), F32),
            pltpu.VMEM((2, 4, 4, 32, 128), BF16),
            pltpu.VMEM((2, 128, 128), BF16),
            pltpu.VMEM((2, 128, 128), BF16),
            pltpu.VMEM((CHIPS, 2, 32, 128), BF16),
            pltpu.VMEM((2, CHIPS, 2, 16, 128), BF16),
            pltpu.VMEM((4, 32, 2, 32, 128), BF16),
            pltpu.VMEM((4, 8, 4, 2, 2, 16, 128), BF16),
            pltpu.VMEM((4, 32, 32, 128), BF16),
            pltpu.VMEM((4, 8, 4, 2, 16, 128), BF16),
            pltpu.VMEM((4, 4, 4, 2, 16, 128), BF16),
            pltpu.VMEM((32, 4, 2, 16, 128), BF16),
            pltpu.VMEM((4, 8, 4, 2, 16, 128), BF16),
            block,
            block,
            pltpu.SemaphoreType.DMA((2,)),
            pltpu.SemaphoreType.DMA((12,)),
            pltpu.SemaphoreType.DMA((2, 2, 4)),
            pltpu.SemaphoreType.DMA((2, 2, 4)),
            pltpu.SemaphoreType.DMA((2,)),
            pltpu.SemaphoreType.DMA((2, 2)),
            pltpu.SemaphoreType.REGULAR((2,)),
            pltpu.SemaphoreType.DMA((9,)),
        ],
        compiler_params=pltpu.CompilerParams(
            collective_id=0, has_side_effects=True, vmem_limit_bytes=56 << 20
        ),
        name="triangles",
    )(pair, in_gain, w_in, out_gain, out_bias, w_out, w_gate_out)


def solution(mesh):
    in_specs = (P("row", "col", None), P(), P(), P(), P(), P(), P())
    out_specs = P("row", "col", None)
    return jax.shard_map(local, mesh=mesh, in_specs=in_specs, out_specs=out_specs, check_vma=False)
```

```python
import jax
import jax.numpy as jnp
from jax import lax
from jax.experimental import pallas as pl
from jax.experimental.pallas import tpu as pltpu
from jax.sharding import PartitionSpec as P

EPS = 1e-05
MESH = pl.DeviceIdType.MESH
CHIPS = 128
BLOCKS = 8
WIDE = 512

F32, BF16 = jnp.float32, jnp.bfloat16


def coordinates():
    row, col = lax.axis_index("row"), lax.axis_index("col")
    return row % 4, (col // 2) % 4, row // 4, col // 8, col % 2


def device(x, y, z_lo, z_hi, core):
    return z_lo * 4 + x, z_hi * 8 + y * 2 + core


def rem(value, by):
    return lax.rem(value, jnp.int32(by))


def div(value, by):
    return lax.div(value, jnp.int32(by))


def sigmoid(values):
    return 0.5 * jnp.tanh(0.5 * values) + 0.5


def norm(values):
    mean = jnp.sum(values, axis=0, keepdims=True) * (1.0 / 128)
    centred = values - mean
    var = jnp.sum(centred * centred, axis=0, keepdims=True) * (1.0 / 128)
    return centred * lax.rsqrt(var + EPS)


def wide(column):
    return jnp.concatenate([column] * (WIDE // 128), axis=1)


def kernel(
    pair, in_gain_hbm, w_in_hbm, out_gain_hbm, out_bias_hbm, w_out_hbm, w_gate_hbm, updated,
    in_gain, w_in, out_gain, out_bias, w_out, w_gate, pair_v, rows, out_rows, z, x_all, gate, staged, gains, wt_in, wt_out, wt_gate,
    ab0, ab1, panel0, panel1, swap_b0, swap_b1, swap_a1, product0, product1, home0, home1,
    send_sems, recv_sems, swap_send, swap_recv, back_send, back_recv, line_sems, local_sems,
):
    bar = pltpu.get_barrier_semaphore()
    x, y, z_lo, z_hi, core = coordinates()
    z_at = z_hi * 2 + z_lo
    col = lax.axis_index("col")
    partner = device(x, y, z_lo, z_hi, 1 - core)
    straight = core == z_lo

    along_y = [device(x, (y + d) % 4, z_lo, z_hi, core) for d in range(1, 4)]
    along_x = [device((x + d) % 4, y, z_lo, z_hi, core) for d in range(1, 4)]

    def greet(sem, devices):
        for to in devices:
            pl.semaphore_signal(sem, inc=1, device_id=to, device_id_type=MESH)

    column = [device(x, y, core, (z_hi + n // 2) % 4, (core + n) % 2) for n in range(8)]
    greet(bar, column[1:])

    @pl.when(straight)
    def _():
        greet(bar, along_y + along_x)

    @pl.when(jnp.logical_not(straight))
    def _():
        greet(bar, along_y + along_x + [column[0], partner])

    arrivals = [
        pltpu.make_async_copy(source, target, local_sems.at[n])
        for n, (source, target) in enumerate(
            (
                (pair, pair_v),
                (w_in_hbm, w_in),
                (in_gain_hbm, in_gain),
                (out_gain_hbm, out_gain),
                (out_bias_hbm, out_bias),
                (w_out_hbm, w_out),
                (w_gate_hbm, w_gate),
            )
        )
    ]
    for copy in arrivals:
        copy.start()

    def flip(block):
        return block.astype(F32).T

    def weights(u):
        for kind in range(4):
            turned = flip(w_in[u, :, 128 * kind : 128 * kind + 128]).astype(BF16)
            wt_in[u, :, kind] = turned.reshape(4, 32, 128)
        gains[3 * u] = jnp.broadcast_to(in_gain[u : u + 1, :], (128, 128)).T

    def late_weights(u):
        wt_out[u] = flip(w_out[u]).astype(BF16)
        wt_gate[u] = flip(w_gate[u]).astype(BF16)
        gains[3 * u + 1] = jnp.broadcast_to(out_gain[u : u + 1, :], (128, 128)).T
        gains[3 * u + 2] = jnp.broadcast_to(out_bias[u : u + 1, :], (128, 128)).T

    def take(t, tokens):
        return rows[pl.ds(t, 128, stride=tokens), :]

    def to_rows(source):
        tokens = source.shape[1]
        some = 512 // tokens

        def part(n, _):
            at = pl.multiple_of(n * 512, 512)
            rows[pl.ds(at, 512), :] = source[pl.ds(n * some, some)].reshape(512, 128).astype(F32)
            return 0

        lax.fori_loop(0, 128 // some, part, 0)

    def projections(u, h, ab, group):
        lhs = wt_in[u, group].reshape(128, 128)
        tokens = ab.shape[2]

        def block(n, _):
            mixed = jnp.dot(lhs, x_all[4 * h + n], preferred_element_type=F32)
            gated = mixed[0:64] * sigmoid(mixed[64:128])
            for kind in range(2):
                for q in range(4):
                    staged[pl.ds(kind * tokens + n * 4 + q, 32, stride=2 * tokens), :] = gated[
                        32 * kind : 32 * kind + 32, 128 * q : 128 * q + 128
                    ]
            return 0

        lax.fori_loop(0, tokens // 4, block, 0)
        some = 128 // tokens

        def pack(d, _):
            at = pl.multiple_of(d * 256, 256)
            ab[pl.ds(group * 32 + d * some, some)] = (
                staged[pl.ds(at, 256), :].astype(BF16).reshape(some, 2, tokens, 128)
            )
            return 0

        lax.fori_loop(0, 32 // some, pack, 0)

    def gates(u):
        def block(n, _):
            gate[n] = sigmoid(jnp.dot(wt_gate[u], x_all[n], preferred_element_type=F32))
            return 0

        lax.fori_loop(0, BLOCKS, block, 0)

    def near(u):
        if u == 0:
            return [(x + d) % 4 for d in (0, 2, 1, 3)]
        return [y, y + 1 - 2 * (y % 2), (y + 2) % 4, 3 - y]

    def forward(u, h, ab, slot, recv):
        inner = y if u == 0 else x
        send = send_sems.at[u]
        for e, to_outer in enumerate(near(u)):
            projections(u, h, ab, to_outer)
            if u == 0 and e == 0:
                pl.semaphore_wait(bar, 14)
                greet(line_sems.at[0], along_y)
            if u == 0 and e == 1:
                pl.semaphore_wait(line_sems.at[1], 3)

            def spread(s, _, to_outer=to_outer, e=e):
                to_inner, to_z = rem(inner + div(s, 8), 4), rem(z_at + 5 * s, 8)
                channel = to_outer * 32 + to_inner * 8 + to_z
                to_x, to_y = (to_outer, to_inner) if u == 0 else (to_inner, to_outer)

                def remote():
                    pltpu.make_async_remote_copy(
                        ab.at[channel],
                        slot,
                        send,
                        recv,
                        device_id=device(to_x, to_y, rem(to_z, 2), div(to_z, 2), z_lo),
                        device_id_type=MESH,
                    ).start()

                if e > 0:
                    remote()
                else:
                    own = jnp.logical_and(s == 0, straight)

                    @pl.when(own)
                    def _():
                        pltpu.make_async_copy(ab.at[channel], slot, recv).start()

                    @pl.when(jnp.logical_not(own))
                    def _():
                        remote()

                return 0

            if u == 0 and e == 0:
                lax.fori_loop(0, 8, spread, 0)
                pl.semaphore_wait(line_sems.at[0], 3)
                greet(line_sems.at[1], along_x)
                lax.fori_loop(8, 32, spread, 0)
            else:
                lax.fori_loop(0, 32, spread, 0)

    def swap(u, chunk, source, target, at):
        return pltpu.make_async_remote_copy(
            source,
            target,
            swap_send.at[u, at, chunk],
            swap_recv.at[u, at, chunk],
            device_id=partner,
            device_id_type=MESH,
        )

    def lanes(parts):
        return jnp.concatenate(parts, axis=1)

    def product_of(right, left, over):
        return lax.dot_general(
            right, left, (((over,), (over,)), ((), ())), preferred_element_type=F32
        ).astype(BF16)

    def multiply0(panel, swap_b, product, home):
        def left(p):
            return lanes([panel[p + 2 * n, :, 0].reshape(1024, 128) for n in range(2)])

        def right(p, side):
            if side == 0:
                return lanes([panel[p + 2 * n, :, 1].reshape(1024, 128) for n in range(2)])
            return lanes([swap_b[p + 2 * n].reshape(1024, 128) for n in range(2)])

        def part(p, q, side):
            out = product_of(right(p, side), left(q), 0)
            half = core if side == 0 else 1 - core
            for n in range(2):
                for m in range(2):
                    product[pl.ds(16 * half + 4 * (p + 2 * n), 4), q + 2 * m] = out[
                        128 * n : 128 * n + 128, 128 * m : 128 * m + 128
                    ].reshape(4, 2, 16, 128)

        def arrive(at):
            pltpu.make_async_copy(panel.at[at], panel.at[at], recv_sems.at[at]).wait()
            copy = swap(0, at, panel.at[at, :, 1], swap_b.at[at], 0)
            copy.start()
            return copy

        p = x % 2
        order = near(0)
        copies = [arrive(at) for at in order[:2]]
        part(p, p, 0)
        for copy in copies:
            copy.wait()
        part(p, p, 1)
        give_back(0, p, product, home, ((0, 0),), (0, 1))
        copies = [arrive(at) for at in order[2:]]
        part(p, 1 - p, 0)
        part(p, 1 - p, 1)
        give_back(0, p, product, home, ((1, 0),), (0,))
        part(1 - p, p, 0)
        part(1 - p, 1 - p, 0)
        for copy in copies:
            copy.wait()
        part(1 - p, p, 1)
        give_back(0, p, product, home, ((0, 1),), (0,))
        part(1 - p, 1 - p, 1)
        give_back(0, p, product, home, ((1, 1),), (0,))
        give_back(0, p, product, home, ((1, 0), (0, 1), (1, 1)), (1,))

    def multiply1(panel, swap_b, swap_a, product, home):
        def left(p):
            def some(source, start):
                return jnp.concatenate(
                    [
                        source(2 * p + m, pl.ds(start + 2 * n, 2)).reshape(64, 128)
                        for n in range(2)
                        for m in range(2)
                    ],
                    axis=0,
                )

            return lanes(
                [some(lambda at, zc: panel[at, zc, n, :, 0], 4 * core) for n in range(4)]
                + [some(lambda at, zc: swap_a[at, zc, n], 0) for n in range(4)]
            )

        def right(at):
            return lanes(
                [panel[at, :, n, :, 1].reshape(256, 128) for n in range(4)]
                + [swap_b[at, :, n].reshape(256, 128) for n in range(4)]
            )

        def part(p, q):
            for m in range(2):
                out = product_of(right(2 * p + m), left(q), 1)
                for n in range(2):
                    product[2 * p + m, :, 2 * n + q] = out[:, 128 * n : 128 * n + 128].reshape(
                        8, 2, 16, 128
                    )

        def arrive(at):
            for h in range(2):
                block = panel.at[at, :, :, h]
                pltpu.make_async_copy(block, block, recv_sems.at[4 + 4 * h + at]).wait()
            copies = [
                swap(1, at, panel.at[at, :, :, :, 1], swap_b.at[at], 0),
                swap(1, at, panel.at[at, pl.ds(4 * (1 - core), 4), :, :, 0], swap_a.at[at], 1),
            ]
            for copy in copies:
                copy.start()
            return copies

        p = y // 2
        order = near(1)
        for copy in arrive(order[0]) + arrive(order[1]):
            copy.wait()
        part(p, p)
        give_back(1, p, product, home, ((0, 0),), (0, 1))
        for copy in arrive(order[2]) + arrive(order[3]):
            copy.wait()
        part(p, 1 - p)
        give_back(1, p, product, home, ((1, 0),), (0,))
        part(1 - p, p)
        give_back(1, p, product, home, ((0, 1),), (0,))
        part(1 - p, 1 - p)
        give_back(1, p, product, home, ((1, 1),), (0,))
        give_back(1, p, product, home, ((1, 0), (0, 1), (1, 1)), (1,))

    def give_back(u, p, product, home, quarters, halves):
        channel = (x * 32 + y * 8 if u == 0 else y * 32 + x * 8) + z_at
        for h in halves:
            for of_x, of_y in quarters:

                def one(s, _, h=h, of_x=of_x, of_y=of_y):
                    to_x = (p + of_x) % 2 + 2 * rem(x // 2 + div(s, 16), 2)
                    to_y = 2 * ((p + of_y) % 2) + rem(y + div(s, 8), 2)
                    to_z, to_core = rem(z_hi + div(s, 2), 4), rem(core + s, 2)
                    to = device(to_x, to_y, core, to_z, to_core)
                    if u == 0:
                        block = product.at[to[1], to_x, h]
                    else:
                        block = product.at[to_y, to_z * 2 + to_core, to_x, h]
                    slot = home.at[h, channel]
                    here = jnp.logical_and(to_x == x, to_y == y)
                    own = jnp.logical_and(jnp.logical_and(rem(s, 8) == 0, straight), here)

                    @pl.when(own)
                    def _():
                        pltpu.make_async_copy(block, slot, back_recv.at[u, h]).start()

                    @pl.when(jnp.logical_not(own))
                    def _():
                        pltpu.make_async_remote_copy(
                            block,
                            slot,
                            back_send.at[u],
                            back_recv.at[u, h],
                            device_id=to,
                            device_id_type=MESH,
                        ).start()

                    return 0

                lax.fori_loop(0, 32, one, 0)

    def received(u, h, home):
        pltpu.make_async_copy(home.at[h], home.at[h], back_recv.at[u, h]).wait()
        to_rows(home.at[h])

    def finish(u, h, n):
        t = lanes([take(n * 4 + q, 16) for q in range(4)])
        tn = norm(t) * wide(gains[3 * u + 1]) + wide(gains[3 * u + 2])
        projected = jnp.dot(wt_out[u], tn.astype(BF16), preferred_element_type=F32)
        return (z[4 * h + n].astype(F32) + projected * gate[4 * h + n]).astype(BF16)

    def enter(u, h, n, block):
        z[4 * h + n] = block
        x_all[4 * h + n] = (norm(block.astype(F32)) * wide(gains[3 * u])).astype(BF16)

    for copy in arrivals[:3]:
        copy.wait()
    weights(0)
    to_rows(pair_v)

    def first(n, _):
        enter(0, 0, n, lanes([take(n * 4 + q, 32).T for q in range(4)]).astype(BF16))
        return 0

    lax.fori_loop(0, BLOCKS, first, 0)
    forward(0, 0, ab0, panel0.at[x, col], recv_sems.at[x])
    for copy in arrivals[3:]:
        copy.wait()
    late_weights(0)
    gates(0)
    weights(1)
    late_weights(1)
    multiply0(panel0, swap_b0, product0, home0)
    for h in range(2):
        received(0, h, home0)

        def second(n, _, h=h):
            enter(1, h, n, finish(0, h, n))
            return 0

        lax.fori_loop(0, 4, second, 0)
        slot = panel1.at[y, z_hi * 2 + core, x, h]
        forward(1, h, ab1.at[h], slot, recv_sems.at[4 + 4 * h + y])
    gates(1)
    multiply1(panel1, swap_b1, swap_a1, product1, home1)
    for h in range(2):
        received(1, h, home1)

        def last(n, _, h=h):
            block = finish(1, h, n).astype(F32)
            for q in range(4):
                staged_out = block[:, 128 * q : 128 * q + 128].T
                out_rows[pl.ds(n * 4 + q, 128, stride=16), :] = staged_out
            return 0

        lax.fori_loop(0, 4, last, 0)

        def leave(n, _, h=h):
            at = pl.multiple_of(n * 512, 512)
            updated[pl.ds(n * 32, 32), 16 * h : 16 * h + 16] = (
                out_rows[pl.ds(at, 512), :].astype(BF16).reshape(32, 16, 128)
            )
            return 0

        lax.fori_loop(0, 4, leave, 0)

    for sent, sem in (
        (ab0, send_sems.at[0]),
        (ab1, send_sems.at[1]),
        (home0, back_send.at[0]),
        (home1, back_send.at[1]),
    ):
        chips = () if sent is ab0 else (slice(None),)
        rest = sent.at[(*chips, pl.ds(0, CHIPS - 1))]
        pltpu.make_async_copy(rest, rest, sem).wait()

        @pl.when(jnp.logical_not(straight))
        def _(sent=sent, sem=sem, chips=chips):
            rest = sent.at[(*chips, 0)]
            pltpu.make_async_copy(rest, rest, sem).wait()


def local(pair, in_gain, w_in, out_gain, out_bias, w_out, w_gate_out):
    anywhere = pl.BlockSpec(memory_space=pl.ANY)
    block = pltpu.VMEM((2, CHIPS, 16, 128), BF16)
    whole = pltpu.VMEM((128, 32, 128), BF16)
    return pl.pallas_call(
        kernel,
        out_shape=pltpu.VMEM(pair.shape, BF16),
        in_specs=[anywhere] * 7,
        out_specs=pl.BlockSpec(memory_space=pltpu.VMEM),
        scratch_shapes=[
            pltpu.VMEM((2, 128), F32),
            pltpu.VMEM((2, 128, 512), BF16),
            pltpu.VMEM((2, 128), F32),
            pltpu.VMEM((2, 128), F32),
            pltpu.VMEM((2, 128, 128), BF16),
            pltpu.VMEM((2, 128, 128), BF16),
            whole,
            pltpu.VMEM((4096, 128), F32),
            pltpu.VMEM((2048, 128), F32),
            pltpu.VMEM((BLOCKS, 128, WIDE), BF16),
            pltpu.VMEM((BLOCKS, 128, WIDE), BF16),
            pltpu.VMEM((BLOCKS, 128, WIDE), F32),
            pltpu.VMEM((2048, 128), F32),
            pltpu.VMEM((6, 128, 128), F32),
            pltpu.VMEM((2, 4, 4, 32, 128), BF16),
            pltpu.VMEM((2, 128, 128), BF16),
            pltpu.VMEM((2, 128, 128), BF16),
            pltpu.VMEM((CHIPS, 2, 32, 128), BF16),
            pltpu.VMEM((2, CHIPS, 2, 16, 128), BF16),
            pltpu.VMEM((4, 32, 2, 32, 128), BF16),
            pltpu.VMEM((4, 8, 4, 2, 2, 16, 128), BF16),
            pltpu.VMEM((4, 32, 32, 128), BF16),
            pltpu.VMEM((4, 8, 4, 2, 16, 128), BF16),
            pltpu.VMEM((4, 4, 4, 2, 16, 128), BF16),
            pltpu.VMEM((32, 4, 2, 16, 128), BF16),
            pltpu.VMEM((4, 8, 4, 2, 16, 128), BF16),
            block,
            block,
            pltpu.SemaphoreType.DMA((2,)),
            pltpu.SemaphoreType.DMA((12,)),
            pltpu.SemaphoreType.DMA((2, 2, 4)),
            pltpu.SemaphoreType.DMA((2, 2, 4)),
            pltpu.SemaphoreType.DMA((2,)),
            pltpu.SemaphoreType.DMA((2, 2)),
            pltpu.SemaphoreType.REGULAR((2,)),
            pltpu.SemaphoreType.DMA((7,)),
        ],
        compiler_params=pltpu.CompilerParams(
            collective_id=0, has_side_effects=True, vmem_limit_bytes=56 << 20
        ),
        name="triangles",
    )(pair, in_gain, w_in, out_gain, out_bias, w_out, w_gate_out)


def solution(mesh):
    in_specs = (P("row", "col", None), P(), P(), P(), P(), P(), P())
    out_specs = P("row", "col", None)
    return jax.shard_map(local, mesh=mesh, in_specs=in_specs, out_specs=out_specs, check_vma=False)
```

```python
import jax
import jax.numpy as jnp
from jax import lax
from jax.experimental import pallas as pl
from jax.experimental.pallas import tpu as pltpu
from jax.sharding import PartitionSpec as P

EPS = 1e-05
MESH = pl.DeviceIdType.MESH
CHIPS = 128
BLOCKS = 8
WIDE = 512

F32, BF16 = jnp.float32, jnp.bfloat16


def coordinates():
    row, col = lax.axis_index("row"), lax.axis_index("col")
    return row % 4, (col // 2) % 4, row // 4, col // 8, col % 2


def device(x, y, z_lo, z_hi, core):
    return z_lo * 4 + x, z_hi * 8 + y * 2 + core


def rem(value, by):
    return lax.rem(value, jnp.int32(by))


def div(value, by):
    return lax.div(value, jnp.int32(by))


def sigmoid(values):
    return 0.5 * jnp.tanh(0.5 * values) + 0.5


def norm(values):
    mean = jnp.sum(values, axis=0, keepdims=True) * (1.0 / 128)
    centred = values - mean
    var = jnp.sum(centred * centred, axis=0, keepdims=True) * (1.0 / 128)
    return centred * lax.rsqrt(var + EPS)


def wide(column):
    return jnp.concatenate([column] * (WIDE // 128), axis=1)


def kernel(
    pair, in_gain_hbm, w_in_hbm, out_gain_hbm, out_bias_hbm, w_out_hbm, w_gate_hbm, updated,
    in_gain, w_in, out_gain, out_bias, w_out, w_gate, pair_v, rows, out_rows, z, x_all, gate, staged, gains, wt_in, wt_out, wt_gate,
    ab0, ab1, panel0, panel1, swap_b0, swap_b1, swap_a1, product0, product1, home0, home1,
    send_sems, recv_sems, swap_send, swap_recv, back_send, back_recv, line_sems, local_sems,
):
    bar = pltpu.get_barrier_semaphore()
    x, y, z_lo, z_hi, core = coordinates()
    z_at = z_hi * 2 + z_lo
    col = lax.axis_index("col")
    partner = device(x, y, z_lo, z_hi, 1 - core)
    straight = core == z_lo

    along_y = [device(x, (y + d) % 4, z_lo, z_hi, core) for d in range(1, 4)]
    along_x = [device((x + d) % 4, y, z_lo, z_hi, core) for d in range(1, 4)]

    def greet(sem, devices):
        for to in devices:
            pl.semaphore_signal(sem, inc=1, device_id=to, device_id_type=MESH)

    column = [device(x, y, core, (z_hi + n // 2) % 4, (core + n) % 2) for n in range(8)]
    greet(bar, column[1:])

    @pl.when(straight)
    def _():
        greet(bar, along_y + along_x)

    @pl.when(jnp.logical_not(straight))
    def _():
        greet(bar, along_y + along_x + [column[0], partner])

    arrivals = [
        pltpu.make_async_copy(source, target, local_sems.at[n])
        for n, (source, target) in enumerate(
            (
                (pair, pair_v),
                (w_in_hbm, w_in),
                (in_gain_hbm, in_gain),
                (out_gain_hbm, out_gain),
                (out_bias_hbm, out_bias),
                (w_out_hbm, w_out),
                (w_gate_hbm, w_gate),
            )
        )
    ]
    for copy in arrivals:
        copy.start()

    def flip(block):
        return block.astype(F32).T

    def weights(u):
        for kind in range(4):
            turned = flip(w_in[u, :, 128 * kind : 128 * kind + 128]).astype(BF16)
            wt_in[u, :, kind] = turned.reshape(4, 32, 128)
        gains[3 * u] = jnp.broadcast_to(in_gain[u : u + 1, :], (128, 128)).T

    def late_weights(u):
        wt_out[u] = flip(w_out[u]).astype(BF16)
        wt_gate[u] = flip(w_gate[u]).astype(BF16)
        gains[3 * u + 1] = jnp.broadcast_to(out_gain[u : u + 1, :], (128, 128)).T
        gains[3 * u + 2] = jnp.broadcast_to(out_bias[u : u + 1, :], (128, 128)).T

    def take(t, tokens):
        return rows[pl.ds(t, 128, stride=tokens), :]

    def to_rows(source):
        tokens = source.shape[1]
        some = 512 // tokens

        def part(n, _):
            at = pl.multiple_of(n * 512, 512)
            rows[pl.ds(at, 512), :] = source[pl.ds(n * some, some)].reshape(512, 128).astype(F32)
            return 0

        lax.fori_loop(0, 128 // some, part, 0)

    def projections(u, h, ab, group):
        lhs = wt_in[u, group].reshape(128, 128)
        tokens = ab.shape[2]

        def block(n, _):
            mixed = jnp.dot(lhs, x_all[4 * h + n], preferred_element_type=F32)
            gated = mixed[0:64] * sigmoid(mixed[64:128])
            for kind in range(2):
                for q in range(4):
                    staged[pl.ds(kind * tokens + n * 4 + q, 32, stride=2 * tokens), :] = gated[
                        32 * kind : 32 * kind + 32, 128 * q : 128 * q + 128
                    ]
            return 0

        lax.fori_loop(0, tokens // 4, block, 0, unroll=2)
        some = 128 // tokens

        def pack(d, _):
            at = pl.multiple_of(d * 256, 256)
            ab[pl.ds(group * 32 + d * some, some)] = (
                staged[pl.ds(at, 256), :].astype(BF16).reshape(some, 2, tokens, 128)
            )
            return 0

        lax.fori_loop(0, 32 // some, pack, 0)

    def gates(u):
        def block(n, _):
            gate[n] = sigmoid(jnp.dot(wt_gate[u], x_all[n], preferred_element_type=F32))
            return 0

        lax.fori_loop(0, BLOCKS, block, 0)

    def near(u):
        if u == 0:
            return [(x + d) % 4 for d in (0, 2, 1, 3)]
        return [y, y + 1 - 2 * (y % 2), (y + 2) % 4, 3 - y]

    def forward(u, h, ab, slot, recv):
        inner = y if u == 0 else x
        send = send_sems.at[u]
        for e, to_outer in enumerate(near(u)):
            projections(u, h, ab, to_outer)
            if u == 0 and e == 0:
                pl.semaphore_wait(bar, 14)
                greet(line_sems.at[0], along_y)
            if u == 0 and e == 1:
                pl.semaphore_wait(line_sems.at[1], 3)

            def spread(s, _, to_outer=to_outer, e=e):
                to_inner, to_z = rem(inner + div(s, 8), 4), rem(z_at + 5 * s, 8)
                channel = to_outer * 32 + to_inner * 8 + to_z
                to_x, to_y = (to_outer, to_inner) if u == 0 else (to_inner, to_outer)

                def remote():
                    pltpu.make_async_remote_copy(
                        ab.at[channel],
                        slot,
                        send,
                        recv,
                        device_id=device(to_x, to_y, rem(to_z, 2), div(to_z, 2), z_lo),
                        device_id_type=MESH,
                    ).start()

                if e > 0:
                    remote()
                else:
                    own = jnp.logical_and(s == 0, straight)

                    @pl.when(own)
                    def _():
                        pltpu.make_async_copy(ab.at[channel], slot, recv).start()

                    @pl.when(jnp.logical_not(own))
                    def _():
                        remote()

                return 0

            if u == 0 and e == 0:
                lax.fori_loop(0, 8, spread, 0)
                pl.semaphore_wait(line_sems.at[0], 3)
                greet(line_sems.at[1], along_x)
                lax.fori_loop(8, 32, spread, 0)
            else:
                lax.fori_loop(0, 32, spread, 0)

    def swap(u, chunk, source, target, at):
        return pltpu.make_async_remote_copy(
            source,
            target,
            swap_send.at[u, at, chunk],
            swap_recv.at[u, at, chunk],
            device_id=partner,
            device_id_type=MESH,
        )

    def lanes(parts):
        return jnp.concatenate(parts, axis=1)

    def product_of(right, left, over):
        return lax.dot_general(
            right, left, (((over,), (over,)), ((), ())), preferred_element_type=F32
        ).astype(BF16)

    def multiply0(panel, swap_b, product, home):
        def left(p):
            return lanes([panel[p + 2 * n, :, 0].reshape(1024, 128) for n in range(2)])

        def right(p, side):
            if side == 0:
                return lanes([panel[p + 2 * n, :, 1].reshape(1024, 128) for n in range(2)])
            return lanes([swap_b[p + 2 * n].reshape(1024, 128) for n in range(2)])

        def part(p, q, side):
            out = product_of(right(p, side), left(q), 0)
            half = core if side == 0 else 1 - core
            for n in range(2):
                for m in range(2):
                    product[pl.ds(16 * half + 4 * (p + 2 * n), 4), q + 2 * m] = out[
                        128 * n : 128 * n + 128, 128 * m : 128 * m + 128
                    ].reshape(4, 2, 16, 128)

        def arrive(at):
            pltpu.make_async_copy(panel.at[at], panel.at[at], recv_sems.at[at]).wait()
            copy = swap(0, at, panel.at[at, :, 1], swap_b.at[at], 0)
            copy.start()
            return copy

        p = x % 2
        order = near(0)
        copies = [arrive(at) for at in order[:2]]
        part(p, p, 0)
        for copy in copies:
            copy.wait()
        part(p, p, 1)
        give_back(0, p, product, home, ((0, 0),), (0, 1))
        copies = [arrive(at) for at in order[2:]]
        part(p, 1 - p, 0)
        part(p, 1 - p, 1)
        give_back(0, p, product, home, ((1, 0),), (0,))
        part(1 - p, p, 0)
        part(1 - p, 1 - p, 0)
        for copy in copies:
            copy.wait()
        part(1 - p, p, 1)
        give_back(0, p, product, home, ((0, 1),), (0,))
        part(1 - p, 1 - p, 1)
        give_back(0, p, product, home, ((1, 1),), (0,))
        give_back(0, p, product, home, ((1, 0), (0, 1), (1, 1)), (1,))

    def multiply1(panel, swap_b, swap_a, product, home):
        def left(p):
            def some(source, start):
                return jnp.concatenate(
                    [
                        source(2 * p + m, pl.ds(start + 2 * n, 2)).reshape(64, 128)
                        for n in range(2)
                        for m in range(2)
                    ],
                    axis=0,
                )

            return lanes(
                [some(lambda at, zc: panel[at, zc, n, :, 0], 4 * core) for n in range(4)]
                + [some(lambda at, zc: swap_a[at, zc, n], 0) for n in range(4)]
            )

        def right(at):
            return lanes(
                [panel[at, :, n, :, 1].reshape(256, 128) for n in range(4)]
                + [swap_b[at, :, n].reshape(256, 128) for n in range(4)]
            )

        def part(p, q):
            for m in range(2):
                out = product_of(right(2 * p + m), left(q), 1)
                for n in range(2):
                    product[2 * p + m, :, 2 * n + q] = out[:, 128 * n : 128 * n + 128].reshape(
                        8, 2, 16, 128
                    )

        def arrive(at):
            for h in range(2):
                block = panel.at[at, :, :, h]
                pltpu.make_async_copy(block, block, recv_sems.at[4 + 4 * h + at]).wait()
            copies = [
                swap(1, at, panel.at[at, :, :, :, 1], swap_b.at[at], 0),
                swap(1, at, panel.at[at, pl.ds(4 * (1 - core), 4), :, :, 0], swap_a.at[at], 1),
            ]
            for copy in copies:
                copy.start()
            return copies

        p = y // 2
        order = near(1)
        for copy in arrive(order[0]) + arrive(order[1]):
            copy.wait()
        part(p, p)
        give_back(1, p, product, home, ((0, 0),), (0, 1))
        for copy in arrive(order[2]) + arrive(order[3]):
            copy.wait()
        part(p, 1 - p)
        give_back(1, p, product, home, ((1, 0),), (0,))
        part(1 - p, p)
        give_back(1, p, product, home, ((0, 1),), (0,))
        part(1 - p, 1 - p)
        give_back(1, p, product, home, ((1, 1),), (0,))
        give_back(1, p, product, home, ((1, 0), (0, 1), (1, 1)), (1,))

    def give_back(u, p, product, home, quarters, halves):
        channel = (x * 32 + y * 8 if u == 0 else y * 32 + x * 8) + z_at
        for h in halves:
            for of_x, of_y in quarters:

                def one(s, _, h=h, of_x=of_x, of_y=of_y):
                    to_x = (p + of_x) % 2 + 2 * rem(x // 2 + div(s, 16), 2)
                    to_y = 2 * ((p + of_y) % 2) + rem(y + div(s, 8), 2)
                    to_z, to_core = rem(z_hi + div(s, 2), 4), rem(core + s, 2)
                    to = device(to_x, to_y, core, to_z, to_core)
                    if u == 0:
                        block = product.at[to[1], to_x, h]
                    else:
                        block = product.at[to_y, to_z * 2 + to_core, to_x, h]
                    slot = home.at[h, channel]
                    here = jnp.logical_and(to_x == x, to_y == y)
                    own = jnp.logical_and(jnp.logical_and(rem(s, 8) == 0, straight), here)

                    @pl.when(own)
                    def _():
                        pltpu.make_async_copy(block, slot, back_recv.at[u, h]).start()

                    @pl.when(jnp.logical_not(own))
                    def _():
                        pltpu.make_async_remote_copy(
                            block,
                            slot,
                            back_send.at[u],
                            back_recv.at[u, h],
                            device_id=to,
                            device_id_type=MESH,
                        ).start()

                    return 0

                lax.fori_loop(0, 32, one, 0)

    def received(u, h, home):
        pltpu.make_async_copy(home.at[h], home.at[h], back_recv.at[u, h]).wait()
        to_rows(home.at[h])

    def finish(u, h, n):
        t = lanes([take(n * 4 + q, 16) for q in range(4)])
        tn = norm(t) * wide(gains[3 * u + 1]) + wide(gains[3 * u + 2])
        projected = jnp.dot(wt_out[u], tn.astype(BF16), preferred_element_type=F32)
        return (z[4 * h + n].astype(F32) + projected * gate[4 * h + n]).astype(BF16)

    def enter(u, h, n, block):
        z[4 * h + n] = block
        x_all[4 * h + n] = (norm(block.astype(F32)) * wide(gains[3 * u])).astype(BF16)

    for copy in arrivals[:3]:
        copy.wait()
    weights(0)
    to_rows(pair_v)

    def first(n, _):
        enter(0, 0, n, lanes([take(n * 4 + q, 32).T for q in range(4)]).astype(BF16))
        return 0

    lax.fori_loop(0, BLOCKS, first, 0, unroll=4)
    forward(0, 0, ab0, panel0.at[x, col], recv_sems.at[x])
    for copy in arrivals[3:]:
        copy.wait()
    late_weights(0)
    gates(0)
    weights(1)
    late_weights(1)
    multiply0(panel0, swap_b0, product0, home0)
    for h in range(2):
        received(0, h, home0)

        def second(n, _, h=h):
            enter(1, h, n, finish(0, h, n))
            return 0

        lax.fori_loop(0, 4, second, 0, unroll=4)
        slot = panel1.at[y, z_hi * 2 + core, x, h]
        forward(1, h, ab1.at[h], slot, recv_sems.at[4 + 4 * h + y])
    gates(1)
    multiply1(panel1, swap_b1, swap_a1, product1, home1)
    for h in range(2):
        received(1, h, home1)

        def last(n, _, h=h):
            block = finish(1, h, n).astype(F32)
            for q in range(4):
                staged_out = block[:, 128 * q : 128 * q + 128].T
                out_rows[pl.ds(n * 4 + q, 128, stride=16), :] = staged_out
            return 0

        lax.fori_loop(0, 4, last, 0, unroll=4)

        def leave(n, _, h=h):
            at = pl.multiple_of(n * 512, 512)
            updated[pl.ds(n * 32, 32), 16 * h : 16 * h + 16] = (
                out_rows[pl.ds(at, 512), :].astype(BF16).reshape(32, 16, 128)
            )
            return 0

        lax.fori_loop(0, 4, leave, 0, unroll=4)

    for sent, sem in (
        (ab0, send_sems.at[0]),
        (ab1, send_sems.at[1]),
        (home0, back_send.at[0]),
        (home1, back_send.at[1]),
    ):
        chips = () if sent is ab0 else (slice(None),)
        rest = sent.at[(*chips, pl.ds(0, CHIPS - 1))]
        pltpu.make_async_copy(rest, rest, sem).wait()

        @pl.when(jnp.logical_not(straight))
        def _(sent=sent, sem=sem, chips=chips):
            rest = sent.at[(*chips, 0)]
            pltpu.make_async_copy(rest, rest, sem).wait()


def local(pair, in_gain, w_in, out_gain, out_bias, w_out, w_gate_out):
    anywhere = pl.BlockSpec(memory_space=pl.ANY)
    block = pltpu.VMEM((2, CHIPS, 16, 128), BF16)
    whole = pltpu.VMEM((128, 32, 128), BF16)
    return pl.pallas_call(
        kernel,
        out_shape=pltpu.VMEM(pair.shape, BF16),
        in_specs=[anywhere] * 7,
        out_specs=pl.BlockSpec(memory_space=pltpu.VMEM),
        scratch_shapes=[
            pltpu.VMEM((2, 128), F32),
            pltpu.VMEM((2, 128, 512), BF16),
            pltpu.VMEM((2, 128), F32),
            pltpu.VMEM((2, 128), F32),
            pltpu.VMEM((2, 128, 128), BF16),
            pltpu.VMEM((2, 128, 128), BF16),
            whole,
            pltpu.VMEM((4096, 128), F32),
            pltpu.VMEM((2048, 128), F32),
            pltpu.VMEM((BLOCKS, 128, WIDE), BF16),
            pltpu.VMEM((BLOCKS, 128, WIDE), BF16),
            pltpu.VMEM((BLOCKS, 128, WIDE), F32),
            pltpu.VMEM((2048, 128), F32),
            pltpu.VMEM((6, 128, 128), F32),
            pltpu.VMEM((2, 4, 4, 32, 128), BF16),
            pltpu.VMEM((2, 128, 128), BF16),
            pltpu.VMEM((2, 128, 128), BF16),
            pltpu.VMEM((CHIPS, 2, 32, 128), BF16),
            pltpu.VMEM((2, CHIPS, 2, 16, 128), BF16),
            pltpu.VMEM((4, 32, 2, 32, 128), BF16),
            pltpu.VMEM((4, 8, 4, 2, 2, 16, 128), BF16),
            pltpu.VMEM((4, 32, 32, 128), BF16),
            pltpu.VMEM((4, 8, 4, 2, 16, 128), BF16),
            pltpu.VMEM((4, 4, 4, 2, 16, 128), BF16),
            pltpu.VMEM((32, 4, 2, 16, 128), BF16),
            pltpu.VMEM((4, 8, 4, 2, 16, 128), BF16),
            block,
            block,
            pltpu.SemaphoreType.DMA((2,)),
            pltpu.SemaphoreType.DMA((12,)),
            pltpu.SemaphoreType.DMA((2, 2, 4)),
            pltpu.SemaphoreType.DMA((2, 2, 4)),
            pltpu.SemaphoreType.DMA((2,)),
            pltpu.SemaphoreType.DMA((2, 2)),
            pltpu.SemaphoreType.REGULAR((2,)),
            pltpu.SemaphoreType.DMA((7,)),
        ],
        compiler_params=pltpu.CompilerParams(
            collective_id=0, has_side_effects=True, vmem_limit_bytes=56 << 20
        ),
        name="triangles",
    )(pair, in_gain, w_in, out_gain, out_bias, w_out, w_gate_out)


def solution(mesh):
    in_specs = (P("row", "col", None), P(), P(), P(), P(), P(), P())
    out_specs = P("row", "col", None)
    return jax.shard_map(local, mesh=mesh, in_specs=in_specs, out_specs=out_specs, check_vma=False)
```

```python
import jax
import jax.numpy as jnp
from jax import lax
from jax.experimental import pallas as pl
from jax.experimental.pallas import tpu as pltpu
from jax.sharding import PartitionSpec as P

EPS = 1e-05
MESH = pl.DeviceIdType.MESH
CHIPS = 128
BLOCKS = 8
WIDE = 512

F32, BF16 = jnp.float32, jnp.bfloat16


def coordinates():
    row, col = lax.axis_index("row"), lax.axis_index("col")
    return row % 4, (col // 2) % 4, row // 4, col // 8, col % 2


def device(x, y, z_lo, z_hi, core):
    return z_lo * 4 + x, z_hi * 8 + y * 2 + core


def rem(value, by):
    return lax.rem(value, jnp.int32(by))


def div(value, by):
    return lax.div(value, jnp.int32(by))


def sigmoid(values):
    return 0.5 * jnp.tanh(0.5 * values) + 0.5


def norm(values):
    mean = jnp.sum(values, axis=0, keepdims=True) * (1.0 / 128)
    centred = values - mean
    var = jnp.sum(centred * centred, axis=0, keepdims=True) * (1.0 / 128)
    return centred * lax.rsqrt(var + EPS)


def wide(column):
    return jnp.concatenate([column] * (WIDE // 128), axis=1)


def kernel(
    pair, in_gain_hbm, w_in_hbm, out_gain_hbm, out_bias_hbm, w_out_hbm, w_gate_hbm, updated,
    in_gain, w_in, out_gain, out_bias, w_out, w_gate, pair_v, rows, out_rows, z, x_all, gate, staged, gains, wt_in, wt_out, wt_gate,
    ab0, ab1, panel0, panel1, swap_b0, swap_b1, swap_a1, product0, product1, home0, home1,
    send_sems, recv_sems, swap_send, swap_recv, back_send, back_recv, line_sems, local_sems,
):
    bar = pltpu.get_barrier_semaphore()
    x, y, z_lo, z_hi, core = coordinates()
    z_at = z_hi * 2 + z_lo
    col = lax.axis_index("col")
    partner = device(x, y, z_lo, z_hi, 1 - core)
    straight = core == z_lo

    along_y = [device(x, (y + d) % 4, z_lo, z_hi, core) for d in range(1, 4)]
    along_x = [device((x + d) % 4, y, z_lo, z_hi, core) for d in range(1, 4)]

    def greet(sem, devices):
        for to in devices:
            pl.semaphore_signal(sem, inc=1, device_id=to, device_id_type=MESH)

    column = [device(x, y, core, (z_hi + n // 2) % 4, (core + n) % 2) for n in range(8)]
    greet(bar, column[1:])

    @pl.when(straight)
    def _():
        greet(bar, along_y + along_x)

    @pl.when(jnp.logical_not(straight))
    def _():
        greet(bar, along_y + along_x + [column[0], partner])

    arrivals = [
        pltpu.make_async_copy(source, target, local_sems.at[n])
        for n, (source, target) in enumerate(
            (
                (pair, pair_v),
                (w_in_hbm, w_in),
                (in_gain_hbm, in_gain),
                (out_gain_hbm, out_gain),
                (out_bias_hbm, out_bias),
                (w_out_hbm, w_out),
                (w_gate_hbm, w_gate),
            )
        )
    ]
    for copy in arrivals:
        copy.start()

    def flip(block):
        return block.astype(F32).T

    def weights(u):
        for kind in range(4):
            turned = flip(w_in[u, :, 128 * kind : 128 * kind + 128]).astype(BF16)
            wt_in[u, :, kind] = turned.reshape(4, 32, 128)
        gains[3 * u] = jnp.broadcast_to(in_gain[u : u + 1, :], (128, 128)).T

    def late_weights(u):
        wt_out[u] = flip(w_out[u]).astype(BF16)
        wt_gate[u] = flip(w_gate[u]).astype(BF16)
        gains[3 * u + 1] = jnp.broadcast_to(out_gain[u : u + 1, :], (128, 128)).T
        gains[3 * u + 2] = jnp.broadcast_to(out_bias[u : u + 1, :], (128, 128)).T

    def take(t, tokens):
        return rows[pl.ds(t, 128, stride=tokens), :]

    def to_rows(source):
        tokens = source.shape[1]
        some = 512 // tokens

        def part(n, _):
            at = pl.multiple_of(n * 512, 512)
            rows[pl.ds(at, 512), :] = source[pl.ds(n * some, some)].reshape(512, 128).astype(F32)
            return 0

        lax.fori_loop(0, 128 // some, part, 0, unroll=2)

    def projections(u, h, ab, group):
        lhs = wt_in[u, group].reshape(128, 128)
        tokens = ab.shape[2]

        def block(n, _):
            mixed = jnp.dot(lhs, x_all[4 * h + n], preferred_element_type=F32)
            gated = mixed[0:64] * sigmoid(mixed[64:128])
            for kind in range(2):
                for q in range(4):
                    staged[pl.ds(kind * tokens + n * 4 + q, 32, stride=2 * tokens), :] = gated[
                        32 * kind : 32 * kind + 32, 128 * q : 128 * q + 128
                    ]
            return 0

        lax.fori_loop(0, tokens // 4, block, 0, unroll=4)
        some = 128 // tokens

        def pack(d, _):
            at = pl.multiple_of(d * 256, 256)
            ab[pl.ds(group * 32 + d * some, some)] = (
                staged[pl.ds(at, 256), :].astype(BF16).reshape(some, 2, tokens, 128)
            )
            return 0

        lax.fori_loop(0, 32 // some, pack, 0)

    def gates(u):
        def block(n, _):
            gate[n] = sigmoid(jnp.dot(wt_gate[u], x_all[n], preferred_element_type=F32))
            return 0

        lax.fori_loop(0, BLOCKS, block, 0)

    def near(u):
        if u == 0:
            return [(x + d) % 4 for d in (0, 2, 1, 3)]
        return [y, y + 1 - 2 * (y % 2), (y + 2) % 4, 3 - y]

    def forward(u, h, ab, slot, recv):
        inner = y if u == 0 else x
        send = send_sems.at[u]
        for e, to_outer in enumerate(near(u)):
            projections(u, h, ab, to_outer)
            if u == 0 and e == 0:
                pl.semaphore_wait(bar, 14)
                greet(line_sems.at[0], along_y)
            if u == 0 and e == 1:
                pl.semaphore_wait(line_sems.at[1], 3)

            def spread(s, _, to_outer=to_outer, e=e):
                to_inner, to_z = rem(inner + div(s, 8), 4), rem(z_at + 5 * s, 8)
                channel = to_outer * 32 + to_inner * 8 + to_z
                to_x, to_y = (to_outer, to_inner) if u == 0 else (to_inner, to_outer)

                def remote():
                    pltpu.make_async_remote_copy(
                        ab.at[channel],
                        slot,
                        send,
                        recv,
                        device_id=device(to_x, to_y, rem(to_z, 2), div(to_z, 2), z_lo),
                        device_id_type=MESH,
                    ).start()

                if e > 0:
                    remote()
                else:
                    own = jnp.logical_and(s == 0, straight)

                    @pl.when(own)
                    def _():
                        pltpu.make_async_copy(ab.at[channel], slot, recv).start()

                    @pl.when(jnp.logical_not(own))
                    def _():
                        remote()

                return 0

            if u == 0 and e == 0:
                lax.fori_loop(0, 8, spread, 0)
                pl.semaphore_wait(line_sems.at[0], 3)
                greet(line_sems.at[1], along_x)
                lax.fori_loop(8, 32, spread, 0)
            else:
                lax.fori_loop(0, 32, spread, 0)

    def swap(u, chunk, source, target, at):
        return pltpu.make_async_remote_copy(
            source,
            target,
            swap_send.at[u, at, chunk],
            swap_recv.at[u, at, chunk],
            device_id=partner,
            device_id_type=MESH,
        )

    def lanes(parts):
        return jnp.concatenate(parts, axis=1)

    def product_of(right, left, over):
        return lax.dot_general(
            right, left, (((over,), (over,)), ((), ())), preferred_element_type=F32
        ).astype(BF16)

    def multiply0(panel, swap_b, product, home):
        def left(p):
            return lanes([panel[p + 2 * n, :, 0].reshape(1024, 128) for n in range(2)])

        def right(p, side):
            if side == 0:
                return lanes([panel[p + 2 * n, :, 1].reshape(1024, 128) for n in range(2)])
            return lanes([swap_b[p + 2 * n].reshape(1024, 128) for n in range(2)])

        def part(p, q, side):
            out = product_of(right(p, side), left(q), 0)
            half = core if side == 0 else 1 - core
            for n in range(2):
                for m in range(2):
                    product[pl.ds(16 * half + 4 * (p + 2 * n), 4), q + 2 * m] = out[
                        128 * n : 128 * n + 128, 128 * m : 128 * m + 128
                    ].reshape(4, 2, 16, 128)

        def arrive(at):
            pltpu.make_async_copy(panel.at[at], panel.at[at], recv_sems.at[at]).wait()
            copy = swap(0, at, panel.at[at, :, 1], swap_b.at[at], 0)
            copy.start()
            return copy

        p = x % 2
        order = near(0)
        copies = [arrive(at) for at in order[:2]]
        part(p, p, 0)
        for copy in copies:
            copy.wait()
        part(p, p, 1)
        give_back(0, p, product, home, ((0, 0),), (0, 1))
        copies = [arrive(at) for at in order[2:]]
        part(p, 1 - p, 0)
        part(p, 1 - p, 1)
        give_back(0, p, product, home, ((1, 0),), (0,))
        part(1 - p, p, 0)
        part(1 - p, 1 - p, 0)
        for copy in copies:
            copy.wait()
        part(1 - p, p, 1)
        give_back(0, p, product, home, ((0, 1),), (0,))
        part(1 - p, 1 - p, 1)
        give_back(0, p, product, home, ((1, 1),), (0,))
        give_back(0, p, product, home, ((1, 0), (0, 1), (1, 1)), (1,))

    def multiply1(panel, swap_b, swap_a, product, home):
        def left(p):
            def some(source, start):
                return jnp.concatenate(
                    [
                        source(2 * p + m, pl.ds(start + 2 * n, 2)).reshape(64, 128)
                        for n in range(2)
                        for m in range(2)
                    ],
                    axis=0,
                )

            return lanes(
                [some(lambda at, zc: panel[at, zc, n, :, 0], 4 * core) for n in range(4)]
                + [some(lambda at, zc: swap_a[at, zc, n], 0) for n in range(4)]
            )

        def right(at):
            return lanes(
                [panel[at, :, n, :, 1].reshape(256, 128) for n in range(4)]
                + [swap_b[at, :, n].reshape(256, 128) for n in range(4)]
            )

        def part(p, q):
            for m in range(2):
                out = product_of(right(2 * p + m), left(q), 1)
                for n in range(2):
                    product[2 * p + m, :, 2 * n + q] = out[:, 128 * n : 128 * n + 128].reshape(
                        8, 2, 16, 128
                    )

        def arrive(at):
            for h in range(2):
                block = panel.at[at, :, :, h]
                pltpu.make_async_copy(block, block, recv_sems.at[4 + 4 * h + at]).wait()
            copies = [
                swap(1, at, panel.at[at, :, :, :, 1], swap_b.at[at], 0),
                swap(1, at, panel.at[at, pl.ds(4 * (1 - core), 4), :, :, 0], swap_a.at[at], 1),
            ]
            for copy in copies:
                copy.start()
            return copies

        p = y // 2
        order = near(1)
        for copy in arrive(order[0]) + arrive(order[1]):
            copy.wait()
        part(p, p)
        give_back(1, p, product, home, ((0, 0),), (0, 1))
        for copy in arrive(order[2]) + arrive(order[3]):
            copy.wait()
        part(p, 1 - p)
        give_back(1, p, product, home, ((1, 0),), (0,))
        part(1 - p, p)
        give_back(1, p, product, home, ((0, 1),), (0,))
        part(1 - p, 1 - p)
        give_back(1, p, product, home, ((1, 1),), (0,))
        give_back(1, p, product, home, ((1, 0), (0, 1), (1, 1)), (1,))

    def give_back(u, p, product, home, quarters, halves):
        channel = (x * 32 + y * 8 if u == 0 else y * 32 + x * 8) + z_at
        for h in halves:
            for of_x, of_y in quarters:

                def one(s, _, h=h, of_x=of_x, of_y=of_y):
                    to_x = (p + of_x) % 2 + 2 * rem(x // 2 + div(s, 16), 2)
                    to_y = 2 * ((p + of_y) % 2) + rem(y + div(s, 8), 2)
                    to_z, to_core = rem(z_hi + div(s, 2), 4), rem(core + s, 2)
                    to = device(to_x, to_y, core, to_z, to_core)
                    if u == 0:
                        block = product.at[to[1], to_x, h]
                    else:
                        block = product.at[to_y, to_z * 2 + to_core, to_x, h]
                    slot = home.at[h, channel]
                    here = jnp.logical_and(to_x == x, to_y == y)
                    own = jnp.logical_and(jnp.logical_and(rem(s, 8) == 0, straight), here)

                    @pl.when(own)
                    def _():
                        pltpu.make_async_copy(block, slot, back_recv.at[u, h]).start()

                    @pl.when(jnp.logical_not(own))
                    def _():
                        pltpu.make_async_remote_copy(
                            block,
                            slot,
                            back_send.at[u],
                            back_recv.at[u, h],
                            device_id=to,
                            device_id_type=MESH,
                        ).start()

                    return 0

                lax.fori_loop(0, 32, one, 0)

    def received(u, h, home):
        pltpu.make_async_copy(home.at[h], home.at[h], back_recv.at[u, h]).wait()
        to_rows(home.at[h])

    def finish(u, h, n):
        t = lanes([take(n * 4 + q, 16) for q in range(4)])
        tn = norm(t) * wide(gains[3 * u + 1]) + wide(gains[3 * u + 2])
        projected = jnp.dot(wt_out[u], tn.astype(BF16), preferred_element_type=F32)
        return (z[4 * h + n].astype(F32) + projected * gate[4 * h + n]).astype(BF16)

    def enter(u, h, n, block):
        z[4 * h + n] = block
        x_all[4 * h + n] = (norm(block.astype(F32)) * wide(gains[3 * u])).astype(BF16)

    for copy in arrivals[:3]:
        copy.wait()
    weights(0)
    to_rows(pair_v)

    def first(n, _):
        enter(0, 0, n, lanes([take(n * 4 + q, 32).T for q in range(4)]).astype(BF16))
        return 0

    lax.fori_loop(0, BLOCKS, first, 0, unroll=4)
    forward(0, 0, ab0, panel0.at[x, col], recv_sems.at[x])
    for copy in arrivals[3:]:
        copy.wait()
    late_weights(0)
    gates(0)
    weights(1)
    late_weights(1)
    multiply0(panel0, swap_b0, product0, home0)
    for h in range(2):
        received(0, h, home0)

        def second(n, _, h=h):
            enter(1, h, n, finish(0, h, n))
            return 0

        lax.fori_loop(0, 4, second, 0, unroll=4)
        slot = panel1.at[y, z_hi * 2 + core, x, h]
        forward(1, h, ab1.at[h], slot, recv_sems.at[4 + 4 * h + y])
    gates(1)
    multiply1(panel1, swap_b1, swap_a1, product1, home1)
    for h in range(2):
        received(1, h, home1)

        def last(n, _, h=h):
            block = finish(1, h, n).astype(F32)
            for q in range(4):
                staged_out = block[:, 128 * q : 128 * q + 128].T
                out_rows[pl.ds(n * 4 + q, 128, stride=16), :] = staged_out
            return 0

        lax.fori_loop(0, 4, last, 0, unroll=4)

        def leave(n, _, h=h):
            at = pl.multiple_of(n * 512, 512)
            updated[pl.ds(n * 32, 32), 16 * h : 16 * h + 16] = (
                out_rows[pl.ds(at, 512), :].astype(BF16).reshape(32, 16, 128)
            )
            return 0

        lax.fori_loop(0, 4, leave, 0, unroll=4)

    for sent, sem in (
        (ab0, send_sems.at[0]),
        (ab1, send_sems.at[1]),
        (home0, back_send.at[0]),
        (home1, back_send.at[1]),
    ):
        chips = () if sent is ab0 else (slice(None),)
        rest = sent.at[(*chips, pl.ds(0, CHIPS - 1))]
        pltpu.make_async_copy(rest, rest, sem).wait()

        @pl.when(jnp.logical_not(straight))
        def _(sent=sent, sem=sem, chips=chips):
            rest = sent.at[(*chips, 0)]
            pltpu.make_async_copy(rest, rest, sem).wait()


def local(pair, in_gain, w_in, out_gain, out_bias, w_out, w_gate_out):
    anywhere = pl.BlockSpec(memory_space=pl.ANY)
    block = pltpu.VMEM((2, CHIPS, 16, 128), BF16)
    whole = pltpu.VMEM((128, 32, 128), BF16)
    return pl.pallas_call(
        kernel,
        out_shape=pltpu.VMEM(pair.shape, BF16),
        in_specs=[anywhere] * 7,
        out_specs=pl.BlockSpec(memory_space=pltpu.VMEM),
        scratch_shapes=[
            pltpu.VMEM((2, 128), F32),
            pltpu.VMEM((2, 128, 512), BF16),
            pltpu.VMEM((2, 128), F32),
            pltpu.VMEM((2, 128), F32),
            pltpu.VMEM((2, 128, 128), BF16),
            pltpu.VMEM((2, 128, 128), BF16),
            whole,
            pltpu.VMEM((4096, 128), F32),
            pltpu.VMEM((2048, 128), F32),
            pltpu.VMEM((BLOCKS, 128, WIDE), BF16),
            pltpu.VMEM((BLOCKS, 128, WIDE), BF16),
            pltpu.VMEM((BLOCKS, 128, WIDE), F32),
            pltpu.VMEM((2048, 128), F32),
            pltpu.VMEM((6, 128, 128), F32),
            pltpu.VMEM((2, 4, 4, 32, 128), BF16),
            pltpu.VMEM((2, 128, 128), BF16),
            pltpu.VMEM((2, 128, 128), BF16),
            pltpu.VMEM((CHIPS, 2, 32, 128), BF16),
            pltpu.VMEM((2, CHIPS, 2, 16, 128), BF16),
            pltpu.VMEM((4, 32, 2, 32, 128), BF16),
            pltpu.VMEM((4, 8, 4, 2, 2, 16, 128), BF16),
            pltpu.VMEM((4, 32, 32, 128), BF16),
            pltpu.VMEM((4, 8, 4, 2, 16, 128), BF16),
            pltpu.VMEM((4, 4, 4, 2, 16, 128), BF16),
            pltpu.VMEM((32, 4, 2, 16, 128), BF16),
            pltpu.VMEM((4, 8, 4, 2, 16, 128), BF16),
            block,
            block,
            pltpu.SemaphoreType.DMA((2,)),
            pltpu.SemaphoreType.DMA((12,)),
            pltpu.SemaphoreType.DMA((2, 2, 4)),
            pltpu.SemaphoreType.DMA((2, 2, 4)),
            pltpu.SemaphoreType.DMA((2,)),
            pltpu.SemaphoreType.DMA((2, 2)),
            pltpu.SemaphoreType.REGULAR((2,)),
            pltpu.SemaphoreType.DMA((7,)),
        ],
        compiler_params=pltpu.CompilerParams(
            collective_id=0, has_side_effects=True, vmem_limit_bytes=56 << 20
        ),
        name="triangles",
    )(pair, in_gain, w_in, out_gain, out_bias, w_out, w_gate_out)


def solution(mesh):
    in_specs = (P("row", "col", None), P(), P(), P(), P(), P(), P())
    out_specs = P("row", "col", None)
    return jax.shard_map(local, mesh=mesh, in_specs=in_specs, out_specs=out_specs, check_vma=False)
```
